128 devices in a mesh: batch: 64 (over z, y, x), feat: 2 (over core).
Axes of the slice: x: 4, y: 4, z: 4, core: 2. Of those that a mesh axis runs over, the one named last changes fastest.
Arguments:
- feature_store: bfloat16 [128, 1048576], P('feat', 'batch'), may hold values from -6 to 6
- requests: int32 [4096, 512], P('batch'), may hold values from 0 to 16383
- block_index: int32 [4096, 8], P('batch'), may hold values from 0 to 511, as said below
- block_values: bfloat16 [4096, 64, 512], P('batch'), may hold values from 0.049804688 to 1
- frontier: int32 [64], P('batch'), may hold values from 1 to 64, as said below
- self_first: bfloat16 [128, 256], replicated, may hold values from -0.5 to 0.5
- neigh_first: bfloat16 [128, 256], replicated, may hold values from -1.1953125 to 1.1953125
- bias_first: float32 [256], replicated, may hold values from -3 to 3
- second_index: int32 [4096, 8], P(('batch', 'feat')), may hold values from 0 to 63
- second_values: bfloat16 [4096, 64, 512], P(('batch', 'feat')), may hold values from 0.049804688 to 1
- self_second: bfloat16 [256, 256], replicated, may hold values from -0.375 to 0.375
- neigh_second: bfloat16 [256, 256], replicated, may hold values from -0.375 to 0.375
- bias_second: float32 [256], replicated, may hold values from -3 to 3
- classifier: bfloat16 [256, 172], replicated, may hold values from -0.375 to 0.375
- bias_class: float32 [172], replicated, may hold values from -3 to 3
Outputs:
- logits: float32 [262144, 172], P(('batch', 'feat'))
The draws below stay inside these ranges and needn't reach their ends.
Inputs may be any that keep to these rules, and one draw needn't show every extreme that they name: `frontier`: exactly one batch group has all 64 target blocks active; the others have between (66) // 3 and 32. `block_index`: within each batch group, the 512 entries of its rows name each of the group's source blocks exactly once.
All inputs are finite; a program needn't handle non-finite values.
Results may differ from the reference program's by a relative error of at most 0.0045.
Values may be sent and summed in bfloat16 or wider, within the bound.
A program may use at most 128 MiB of HBM per device.

```python
import jax
import jax.numpy as jnp
from jax import lax

FEAT = 128
HID = 256
CLASSES = 172
BLOCK = 64
NBR = 8
NBR2 = 8
TB = 64
STORE_DEV = 16384
CAP = 512
NODES = 1048576
ALL_TB = 4096
REQ_ROWS = 4096
N_BATCH = 64


def draw_frontier(key, part):
    key = jax.random.fold_in(key, 11)
    first_key, second_key = jax.random.split(key)
    lowest = max(1, (TB + 2) // 3)
    common = jax.random.randint(first_key, (N_BATCH,), lowest, TB // 2 + 1)
    busiest = jax.random.randint(second_key, (), 0, N_BATCH)
    filled = jnp.where(jnp.arange(N_BATCH) == busiest, TB, common)
    return filled.astype(jnp.int32)


def draw_block_index(key, part):
    key = jax.random.fold_in(key, 5)
    group_keys = jax.random.split(key, N_BATCH)

    def one_order(group_key):
        return jax.random.permutation(group_key, TB * NBR)
    orders = jax.vmap(one_order)(group_keys)
    return orders.reshape(N_BATCH * TB, NBR).astype(jnp.int32)


def place_ends(values, stream_key, low, largest):
    longest = values.shape.index(max(values.shape))
    spots = []
    for shift in (0, 1):
        where = [jax.random.randint(jax.random.fold_in(stream_key, axis), (), 0, length) for axis, length in enumerate(values.shape)]
        where[longest] = (where[longest] + shift) % values.shape[longest]
        spots.append(tuple(where))
    return values.at[spots[0]].set(low).at[spots[1]].set(largest)


def steps_of(own_key, extent, shards, least, top_value):
    loudness = 1.0
    for axis_at, shards_of in shards:
        steps = jax.random.uniform(jax.random.fold_in(jax.random.fold_in(own_key, 6), axis_at), (shards_of,), jnp.float32, least / len(shards), top_value / len(shards))
        loudness = loudness * jnp.repeat(jnp.exp(steps), extent[axis_at] // shards_of).reshape((-1,) + (1,) * (len(extent) - 1 - axis_at))
    return loudness


def noise(own_key, shape, spread, most, shards=(), kind=jnp.bfloat16):
    level = steps_of(own_key, shape, shards, -0.22, 0.18) if shards else 1.0
    values = jax.random.normal(own_key, shape, jnp.float32) * spread * level
    return jnp.minimum(jnp.maximum(values, -most), most).astype(kind)


def setup_inputs(seed: int = 0) -> dict:
    streams_of = jax.random.split(jax.random.key(seed), 16)
    feature_store = noise(streams_of[0], (FEAT, NODES), 1.0, 6.0, ((0, 2), (1, 64)))
    requests = place_ends(jax.random.randint(streams_of[1], (REQ_ROWS, CAP), 0, STORE_DEV), jax.random.fold_in(streams_of[1], 1), 0, STORE_DEV - 1).astype(jnp.int32)
    block_index = draw_block_index(jax.random.fold_in(streams_of[15], 71), 0)
    block_values = jnp.clip(0.049804688 + 0.9501953 * jax.random.uniform(streams_of[3], (ALL_TB, BLOCK, NBR * BLOCK), jnp.float32) ** steps_of(streams_of[3], (ALL_TB, BLOCK, NBR * BLOCK), ((0, 64),), -0.2, 0.2), 0.049804688, 1.0).astype(jnp.bfloat16)
    frontier = draw_frontier(jax.random.fold_in(streams_of[15], 71), 0)
    self_first = noise(streams_of[5], (FEAT, HID), FEAT ** -0.5, 0.5)
    neigh_first = noise(streams_of[6], (FEAT, HID), 0.2, 1.1953125)
    bias_first = noise(streams_of[7], (HID,), 0.5, 3.0, (), jnp.float32)
    second_index = place_ends(jax.random.randint(streams_of[8], (ALL_TB, NBR2), 0, TB), jax.random.fold_in(streams_of[8], 1), 0, TB - 1).astype(jnp.int32)
    second_values = jnp.clip(0.049804688 + 0.9501953 * jax.random.uniform(streams_of[9], (ALL_TB, BLOCK, NBR2 * BLOCK), jnp.float32) ** steps_of(streams_of[9], (ALL_TB, BLOCK, NBR2 * BLOCK), ((0, 128),), -0.2, 0.2), 0.049804688, 1.0).astype(jnp.bfloat16)
    self_second = noise(streams_of[10], (HID, HID), HID ** -0.5, 0.375)
    neigh_second = noise(streams_of[11], (HID, HID), HID ** -0.5, 0.375)
    bias_second = noise(streams_of[12], (HID,), 0.5, 3.0, (), jnp.float32)
    classifier = noise(streams_of[13], (HID, CLASSES), HID ** -0.5, 0.375)
    bias_class = noise(streams_of[14], (CLASSES,), 0.5, 3.0, (), jnp.float32)
    return {"feature_store": feature_store, "requests": requests, "block_index": block_index, "block_values": block_values, "frontier": frontier, "self_first": self_first, "neigh_first": neigh_first, "bias_first": bias_first, "second_index": second_index, "second_values": second_values, "self_second": self_second, "neigh_second": neigh_second, "bias_second": bias_second, "classifier": classifier, "bias_class": bias_class}


def reference(feature_store, requests, block_index, block_values, frontier, self_first, neigh_first, bias_first, second_index, second_values, self_second, neigh_second, bias_second, classifier, bias_class):
    groups = N_BATCH
    wanted = requests.reshape(groups, groups, CAP)
    offsets = (jnp.arange(groups, dtype=jnp.int32) * STORE_DEV)[None, :, None]
    columns_all = (wanted + offsets).astype(jnp.int32).reshape(groups, groups * CAP)
    index_one = block_index.reshape(groups, TB, NBR)
    values_one = block_values.reshape(groups, TB, BLOCK, NBR * BLOCK)
    index_two = second_index.reshape(groups, TB, NBR2)
    values_two = second_values.reshape(groups, TB, BLOCK, NBR2 * BLOCK)
    contract = (((0,), (0,)), ((), ()))

    def one_group(items):
        columns, index, values, index_b, values_b, limit = items
        sources = jnp.take(feature_store, columns, axis=1)
        tiled = sources.reshape(FEAT, -1, BLOCK)
        chosen = jnp.take(tiled, index, axis=1).astype(jnp.float32).reshape(FEAT, TB, NBR * BLOCK)
        weights = values.astype(jnp.float32)
        summed = jnp.einsum("ctm,tim->cti", chosen, weights)
        totals = jnp.sum(weights, axis=2)
        aggregated = (summed / totals[None]).astype(jnp.bfloat16).reshape(FEAT, TB * BLOCK)
        own_self = sources[:, :TB * BLOCK]
        pre_first = lax.dot_general(own_self, self_first, contract, preferred_element_type=jnp.float32) + lax.dot_general(aggregated, neigh_first, contract, preferred_element_type=jnp.float32) + bias_first
        active = (jnp.arange(TB * BLOCK, dtype=jnp.int32) // BLOCK) < limit
        layer_one = jnp.where(active[:, None], jnp.maximum(pre_first, 0.0), 0.0).astype(jnp.bfloat16)
        tiles = layer_one.reshape(TB, BLOCK, HID)
        chosen_two = jnp.take(tiles, index_b, axis=0).astype(jnp.float32).reshape(TB, NBR2 * BLOCK, HID)
        weights_two = values_b.astype(jnp.float32)
        summed_two = jnp.einsum("tim,tmh->tih", weights_two, chosen_two)
        totals_two = jnp.sum(weights_two, axis=2)
        aggregated_two = (summed_two / totals_two[..., None]).astype(jnp.bfloat16).reshape(TB * BLOCK, HID)
        pre_second = jnp.dot(layer_one, self_second, preferred_element_type=jnp.float32) + jnp.dot(aggregated_two, neigh_second, preferred_element_type=jnp.float32) + bias_second
        layer_two = jnp.where(active[:, None], jnp.maximum(pre_second, 0.0), 0.0).astype(jnp.bfloat16)
        return jnp.dot(layer_two, classifier, preferred_element_type=jnp.float32) + bias_class

    result = lax.map(one_group, (columns_all, index_one, values_one, index_two, values_two, frontier))
    return result.reshape(groups * TB * BLOCK, CLASSES)
```

```python
import functools

import jax
import jax.numpy as jnp
from jax import lax
from jax.experimental import pallas as pl
from jax.experimental.pallas import tpu as pltpu
from jax.sharding import PartitionSpec as P

MESH = pl.DeviceIdType.MESH
BLOCK = 64
GROUPS = 64
HALF_CAP = 256
FEAT = 128
HID = 256
TB = 64
OWN_TB = 32
NBR = 8
STORE = 16384
CHUNKS = 4
ROW_CHUNKS = 8


def torus_order():
    def orbit(t):
        z, y, x = t
        found = []
        for r in ((z, y, x), (y, x, z), (x, z, y)):
            for n in (r, tuple((-v) % 4 for v in r)):
                if n not in found:
                    found.append(n)
        return found

    seen, orbits = set(), []
    for s in range(1, GROUPS):
        t = (s // 16, (s // 4) % 4, s % 4)
        if t not in seen:
            o = orbit(t)
            seen.update(o)
            orbits.append(o)
    left = sorted(orbits, key=lambda o: -sum(min(d, 4 - d) for d in o[0]))
    mixed = []
    while left:
        mixed.append(left.pop(0))
        if left:
            mixed.append(left.pop())
    return [t[0] * 16 + t[1] * 4 + t[2] for o in mixed for t in o]


ORDER = torus_order()
WORDS = [
    sum(s * 64**e for e, s in enumerate(ORDER[w : w + 5])) for w in range(0, GROUPS - 1, 5)
]


def shift_of(i):
    word = jnp.int32(WORDS[0])
    for w in range(1, len(WORDS)):
        word = jnp.where(i // 5 == w, jnp.int32(WORDS[w]), word)
    place = lax.rem(i, 5)
    shift = lax.rem(word, 64)
    for e in range(1, 5):
        shift = jnp.where(place == e, lax.rem(word // 64**e, 64), shift)
    return shift


def peer(me, s):
    z, y, x = me // 16, (me // 4) % 4, me % 4
    dz, dy, dx = s // 16, (s // 4) % 4, s % 4
    return ((z + dz) % 4) * 16 + ((y + dy) % 4) * 4 + (x + dx) % 4


def first_kernel(
    store_hbm,
    req,
    places,
    mine,
    values_hbm,
    frontier,
    w_self,
    w_neigh,
    bias,
    out,
    cols,
    rows,
    sreq,
    rreq,
    idx,
    tmp,
    sendbuf,
    rbuf,
    values,
    psend,
    precv,
    totals,
    selfbuf,
    agg,
    chosen,
    l1,
    load_sem,
    half_send,
    half_recv,
    req_send,
    req_recv,
    idx_sem,
    msg_send,
    msg_recv,
    p_send,
    p_recv,
    self_send,
    self_recv,
    self_own,
    l1_send,
    l1_recv,
    l1_own,
):
    me = lax.axis_index("batch")
    c = lax.axis_index("feat")
    sib = 1 - c

    barrier = pltpu.get_barrier_semaphore()
    pl.semaphore_signal(barrier, inc=1, device_id=(me, sib), device_id_type=MESH)

    def greet(s, _):
        pl.semaphore_signal(
            barrier, inc=1, device_id=(lax.rem(me + s, GROUPS), c), device_id_type=MESH
        )
        return 0

    lax.fori_loop(1, GROUPS, greet, 0)

    width = STORE // CHUNKS
    half = pl.ds(pl.multiple_of(c * 64, 64), 64)
    own_load = pltpu.make_async_copy(store_hbm, cols.at[half], load_sem.at[0])
    own_load.start()
    values_load = pltpu.make_async_copy(values_hbm, values, load_sem.at[1])
    values_load.start()
    for h in range(2):
        sreq[:, h, :] = req[:, pl.ds(pl.multiple_of(c * HALF_CAP + h * 128, 128), 128)]
    rreq[me] = sreq[me]
    pl.semaphore_wait(barrier, GROUPS)

    def req_copy(s):
        p = lax.rem(me + s, GROUPS)
        return pltpu.make_async_remote_copy(
            src_ref=sreq.at[p],
            dst_ref=rreq.at[me],
            send_sem=req_send.at[s],
            recv_sem=req_recv.at[s],
            device_id=(p, c),
            device_id_type=MESH,
        )

    def req_start(s, _):
        req_copy(s).start()
        return 0

    lax.fori_loop(1, GROUPS, req_start, 0)

    def half_copy(j):
        part = pl.ds(j * width, width)
        return pltpu.make_async_remote_copy(
            src_ref=store_hbm.at[:, part],
            dst_ref=cols.at[half, part],
            send_sem=half_send.at[j],
            recv_sem=half_recv.at[j],
            device_id=(me, sib),
            device_id_type=MESH,
        )

    for j in range(CHUNKS):
        half_copy(j).start()
    own_load.wait()
    for j in range(CHUNKS):
        half_copy(j).wait_recv()

        def turn(i, _):
            at = pl.multiple_of(j * width + i * 512, 512)
            rows[pl.ds(at, 512), :] = cols[:, pl.ds(at, 512)].T.astype(jnp.float32)
            return 0

        lax.fori_loop(0, width // 512, turn, 0)

    def req_wait(s, _):
        req_copy(s).wait_recv()
        return 0

    lax.fori_loop(1, GROUPS, req_wait, 0)
    idx_copy = pltpu.make_async_copy(rreq, idx, idx_sem)
    idx_copy.start()
    idx_copy.wait()

    def gather(p):
        for h in range(2):
            for q in range(128):
                tmp[pl.ds(h * 128 + q, 1), :] = rows[pl.ds(idx[p, h, q], 1), :]
        return tmp[...].astype(jnp.bfloat16).reshape(4, BLOCK, FEAT)

    def msg_copy(s):
        p = peer(me, s)
        return pltpu.make_async_remote_copy(
            src_ref=sendbuf.at[pl.ds(p * 4, 4)],
            dst_ref=rbuf.at[pl.ds(me * 4, 4)],
            send_sem=msg_send.at[s],
            recv_sem=msg_recv.at[s],
            device_id=(p, c),
            device_id_type=MESH,
        )

    def msg_start(i, _):
        s = shift_of(i)
        p = peer(me, s)
        sendbuf[pl.ds(p * 4, 4)] = gather(p)
        msg_copy(s).start()
        return 0

    lax.fori_loop(0, GROUPS - 1, msg_start, 0)
    rbuf[pl.ds(me * 4, 4)] = gather(me)

    values_load.wait()
    ones = jnp.ones((512, FEAT), jnp.bfloat16)

    def total(t, _):
        totals[t] = jnp.dot(values[c * OWN_TB + t], ones, preferred_element_type=jnp.float32)
        return 0

    lax.fori_loop(0, OWN_TB, total, 0)

    def msg_wait(s, _):
        msg_copy(s).wait_recv()
        return 0

    lax.fori_loop(1, GROUPS, msg_wait, 0)

    def self_copy(j):
        return pltpu.make_async_remote_copy(
            src_ref=rbuf.at[pl.ds((sib * 4 + j) * 4, 4)],
            dst_ref=selfbuf.at[2 * j + c],
            send_sem=self_send.at[j],
            recv_sem=self_recv.at[j],
            device_id=(me, sib),
            device_id_type=MESH,
        )

    def self_local(j):
        return pltpu.make_async_copy(
            rbuf.at[pl.ds((c * 4 + j) * 4, 4)], selfbuf.at[2 * j + c], self_own.at[j]
        )

    for j in range(4):
        self_copy(j).start()
        self_local(j).start()

    def partial_sum(t, slot):
        for k in range(NBR):
            chosen[slot, pl.ds(k * BLOCK, BLOCK), :] = rbuf[places[t, k]]
        weights = values[t] * mine[pl.ds(t, 1), :].astype(jnp.bfloat16)
        return jnp.dot(weights, chosen[slot], preferred_element_type=jnp.float32)

    def p_copy(m):
        return pltpu.make_async_remote_copy(
            src_ref=psend.at[pl.ds(m * 8, 8)],
            dst_ref=precv.at[pl.ds(m * 8, 8)],
            send_sem=p_send.at[m],
            recv_sem=p_recv.at[m],
            device_id=(me, sib),
            device_id_type=MESH,
        )

    for m in range(4):

        def other(i, _):
            for u in range(4):
                t = m * 8 + i * 4 + u
                psend[t] = partial_sum(sib * OWN_TB + t, u)
            return 0

        lax.fori_loop(0, 2, other, 0)
        p_copy(m).start()

    def own(i, _):
        for u in range(4):
            t = i * 4 + u
            agg[t] = partial_sum(c * OWN_TB + t, u)
        return 0

    lax.fori_loop(0, OWN_TB // 4, own, 0)

    def l1_copy(m):
        at = pl.multiple_of(c * 2048 + m * 256, 256)
        return pltpu.make_async_remote_copy(
            src_ref=l1.at[pl.ds(m * 256, 256)],
            dst_ref=out.at[pl.ds(at, 256)],
            send_sem=l1_send.at[m],
            recv_sem=l1_recv.at[m],
            device_id=(me, sib),
            device_id_type=MESH,
        )

    def l1_local(m):
        at = pl.multiple_of(c * 2048 + m * 256, 256)
        return pltpu.make_async_copy(
            l1.at[pl.ds(m * 256, 256)], out.at[pl.ds(at, 256)], l1_own.at[m]
        )

    for j in range(4):
        self_copy(j).wait_recv()
        self_local(j).wait()
    for m in range(ROW_CHUNKS):
        if m % 2 == 0:
            p_copy(m // 2).wait_recv()
        mean = (agg[pl.ds(m * 4, 4)] + precv[pl.ds(m * 4, 4)]) / totals[pl.ds(m * 4, 4)]
        mean = mean.astype(jnp.bfloat16).reshape(256, FEAT)
        pre = (
            jnp.dot(selfbuf[m].reshape(256, FEAT), w_self[...], preferred_element_type=jnp.float32)
            + jnp.dot(mean, w_neigh[...], preferred_element_type=jnp.float32)
            + bias[...]
        )
        number = c * OWN_TB + m * 4 + lax.broadcasted_iota(jnp.int32, (256, HID), 0) // BLOCK
        layer = jnp.where(number < frontier[0], jnp.maximum(pre, 0.0), 0.0)
        l1[pl.ds(m * 256, 256), :] = layer.astype(jnp.bfloat16)
        l1_copy(m).start()
        l1_local(m).start()

    for m in range(ROW_CHUNKS):
        l1_copy(m).wait()
        l1_local(m).wait()
    for j in range(CHUNKS):
        half_copy(j).wait_send()
    for j in range(4):
        self_copy(j).wait_send()
        p_copy(j).wait_send()

    def sent(s, _):
        req_copy(s).wait_send()
        msg_copy(s).wait_send()
        return 0

    lax.fori_loop(1, GROUPS, sent, 0)


def second_kernel(
    rows, second_index, frontier, values, w_self, w_neigh, bias, w_class, bias_class, out, chosen
):
    m = pl.program_id(0)
    c = lax.axis_index("feat")
    ones = jnp.ones((512, 128), jnp.bfloat16)
    means = []
    for u in range(4):
        for k in range(NBR):
            at = pl.multiple_of(second_index[m * 4 + u, k] * BLOCK, BLOCK)
            chosen[u, pl.ds(k * BLOCK, BLOCK), :] = rows[pl.ds(at, BLOCK), :]
        summed = jnp.dot(values[u], chosen[u], preferred_element_type=jnp.float32)
        total = jnp.dot(values[u], ones, preferred_element_type=jnp.float32)
        total = jnp.concatenate([total, total], axis=1)
        means.append((summed / total).astype(jnp.bfloat16))
    mean = jnp.concatenate(means, axis=0)
    own = rows[pl.ds(pl.multiple_of(c * 2048 + m * 256, 256), 256), :]
    pre = (
        jnp.dot(own, w_self[...], preferred_element_type=jnp.float32)
        + jnp.dot(mean, w_neigh[...], preferred_element_type=jnp.float32)
        + bias[...]
    )
    number = c * OWN_TB + m * 4 + lax.broadcasted_iota(jnp.int32, (256, HID), 0) // BLOCK
    layer = jnp.where(number < frontier[0], jnp.maximum(pre, 0.0), 0.0).astype(jnp.bfloat16)
    out[...] = (
        lax.dot_general(
            w_class[...], layer, (((1,), (1,)), ((), ())), preferred_element_type=jnp.float32
        )
        + bias_class[...]
    )


def body(
    feature_store,
    requests,
    block_index,
    block_values,
    frontier,
    self_first,
    neigh_first,
    bias_first,
    second_index,
    second_values,
    self_second,
    neigh_second,
    bias_second,
    classifier,
    bias_class,
):
    vmem = pl.BlockSpec(memory_space=pltpu.VMEM)
    smem = pl.BlockSpec(memory_space=pltpu.SMEM)
    hbm = pl.BlockSpec(memory_space=pl.ANY)
    dma = pltpu.SemaphoreType.DMA
    bf16, f32, i32 = jnp.bfloat16, jnp.float32, jnp.int32
    places = block_index // 8 * 4 + block_index % 4
    held = (block_index // 4 % 2 == lax.axis_index("feat")).astype(f32)
    mine = jnp.repeat(held, BLOCK, axis=1)
    layer_one = pl.pallas_call(
        first_kernel,
        out_shape=jax.ShapeDtypeStruct((TB * BLOCK, HID), bf16),
        in_specs=[hbm, vmem, smem, vmem, hbm, smem, vmem, vmem, vmem],
        out_specs=hbm,
        scratch_shapes=[
            pltpu.VMEM((FEAT, STORE), bf16),
            pltpu.VMEM((STORE, FEAT), f32),
            pltpu.VMEM((GROUPS, 2, 128), i32),
            pltpu.VMEM((GROUPS, 2, 128), i32),
            pltpu.SMEM((GROUPS, 2, 128), i32),
            pltpu.VMEM((HALF_CAP, FEAT), f32),
            pltpu.VMEM((GROUPS * 4, BLOCK, FEAT), bf16),
            pltpu.VMEM((GROUPS * 4, BLOCK, FEAT), bf16),
            pltpu.VMEM((TB, BLOCK, NBR * BLOCK), bf16),
            pltpu.VMEM((OWN_TB, BLOCK, FEAT), f32),
            pltpu.VMEM((OWN_TB, BLOCK, FEAT), f32),
            pltpu.VMEM((OWN_TB, BLOCK, FEAT), f32),
            pltpu.VMEM((8, 4, BLOCK, FEAT), bf16),
            pltpu.VMEM((OWN_TB, BLOCK, FEAT), f32),
            pltpu.VMEM((4, NBR * BLOCK, FEAT), bf16),
            pltpu.VMEM((OWN_TB * BLOCK, HID), bf16),
            dma((2,)),
            dma((CHUNKS,)),
            dma((CHUNKS,)),
            dma((GROUPS,)),
            dma((GROUPS,)),
            dma,
            dma((GROUPS,)),
            dma((GROUPS,)),
            dma((4,)),
            dma((4,)),
            dma((4,)),
            dma((4,)),
            dma((4,)),
            dma((ROW_CHUNKS,)),
            dma((ROW_CHUNKS,)),
            dma((ROW_CHUNKS,)),
        ],
        compiler_params=pltpu.CompilerParams(
            collective_id=0, has_side_effects=True, vmem_limit_bytes=48 * 2**20
        ),
        name="layer_one",
    )(
        feature_store,
        requests,
        places,
        mine,
        block_values,
        frontier,
        self_first,
        neigh_first,
        bias_first.reshape(1, HID),
    )
    classes = classifier.shape[1]
    whole = lambda *shape: pl.BlockSpec(shape, lambda m: (0,) * len(shape))
    logits = pl.pallas_call(
        second_kernel,
        grid=(ROW_CHUNKS,),
        out_shape=jax.ShapeDtypeStruct((classes, OWN_TB * BLOCK), f32),
        in_specs=[
            whole(TB * BLOCK, HID),
            smem,
            smem,
            pl.BlockSpec((4, BLOCK, NBR * BLOCK), lambda m: (m, 0, 0)),
            whole(HID, HID),
            whole(HID, HID),
            whole(1, HID),
            whole(classes, HID),
            whole(classes, 1),
        ],
        out_specs=pl.BlockSpec((classes, 256), lambda m: (0, m)),
        scratch_shapes=[pltpu.VMEM((4, NBR * BLOCK, HID), bf16)],
        compiler_params=pltpu.CompilerParams(vmem_limit_bytes=32 * 2**20),
        name="layer_two",
    )(
        layer_one,
        second_index,
        frontier,
        second_values,
        self_second,
        neigh_second,
        bias_second.reshape(1, HID),
        classifier.T,
        bias_class.reshape(classes, 1),
    )
    return logits.T


def solution(mesh):
    in_specs = (
        P("feat", "batch"),
        P("batch", None),
        P("batch", None),
        P("batch", None, None),
        P("batch"),
        P(),
        P(),
        P(),
        P(("batch", "feat"), None),
        P(("batch", "feat"), None, None),
        P(),
        P(),
        P(),
        P(),
        P(),
    )
    out_specs = P(("batch", "feat"), None)
    return jax.shard_map(body, mesh=mesh, in_specs=in_specs, out_specs=out_specs, check_vma=False)
```

```python
import functools

import jax
import jax.numpy as jnp
from jax import lax
from jax.experimental import pallas as pl
from jax.experimental.pallas import tpu as pltpu
from jax.sharding import PartitionSpec as P

MESH = pl.DeviceIdType.MESH
BLOCK = 64
GROUPS = 64
HALF_CAP = 256
FEAT = 128
HID = 256
TB = 64
OWN_TB = 32
NBR = 8
STORE = 16384
CHUNKS = 4
ROW_CHUNKS = 8


ORDER = (
    42, 54, 28, 4, 46, 61, 23, 34, 8, 59, 17, 6, 44, 45, 7, 50,
    24, 29, 55, 30, 52, 47, 5, 13, 39, 58, 16, 1, 43, 62, 20, 2,
    40, 41, 3, 15, 37, 18, 56, 63, 21, 11, 33, 48, 26, 12, 38, 36,
    14, 53, 31, 22, 60, 10, 32, 35, 9, 19, 57, 51, 25, 27, 49,
)
WORDS = [
    sum(s * 64**e for e, s in enumerate(ORDER[w : w + 5])) for w in range(0, GROUPS - 1, 5)
]


def shift_of(i):
    word = jnp.int32(WORDS[0])
    for w in range(1, len(WORDS)):
        word = jnp.where(i // 5 == w, jnp.int32(WORDS[w]), word)
    place = lax.rem(i, 5)
    shift = lax.rem(word, 64)
    for e in range(1, 5):
        shift = jnp.where(place == e, lax.rem(word // 64**e, 64), shift)
    return shift


def peer(me, s, c):
    z, y, x = me // 16, (me // 4) % 4, me % 4
    dz, dy, dx = s // 16, (s // 4) % 4, s % 4
    dz, dy, dx = (lax.rem(d * (1 + 2 * c), 4) for d in (dz, dy, dx))
    return ((z + dz) % 4) * 16 + ((y + dy) % 4) * 4 + (x + dx) % 4


def kernel(
    store_hbm,
    req_hbm,
    index_hbm,
    values_hbm,
    frontier,
    w_self_hbm,
    w_neigh_hbm,
    bias_hbm,
    index_two_hbm,
    values_two_hbm,
    w_self_two_hbm,
    w_neigh_two_hbm,
    bias_two_hbm,
    out,
    cols,
    rows,
    req,
    sreq,
    rreq,
    idx,
    index_vec,
    index,
    index_two,
    tmp,
    sendbuf,
    rbuf,
    values,
    values_two,
    held,
    w_self,
    w_neigh,
    bias,
    w_self_two,
    w_neigh_two,
    bias_two,
    psend,
    precv,
    totals,
    totals_two,
    selfbuf,
    agg,
    l1,
    pre_two,
    l2,
    load_sem,
    half_send,
    half_recv,
    req_send,
    req_recv,
    idx_sem,
    msg_send,
    msg_recv,
    p_send,
    p_recv,
    self_send,
    self_recv,
    self_own,
    l1_send,
    l1_recv,
    out_sem,
):
    me = lax.axis_index("batch")
    c = lax.axis_index("feat")
    sib = 1 - c
    f32, bf16 = jnp.float32, jnp.bfloat16

    barrier = pltpu.get_barrier_semaphore()
    pl.semaphore_signal(barrier, inc=1, device_id=(me, sib), device_id_type=MESH)

    def greet(s, _):
        pl.semaphore_signal(
            barrier, inc=1, device_id=(lax.rem(me + s, GROUPS), c), device_id_type=MESH
        )
        return 0

    lax.fori_loop(1, GROUPS, greet, 0)

    half = pl.ds(pl.multiple_of(c * 64, 64), 64)
    loads = [
        pltpu.make_async_copy(src, dst, load_sem.at[i])
        for i, (src, dst) in enumerate(
            (
                (req_hbm, req),
                (store_hbm, cols.at[half]),
                (index_hbm, index_vec),
                (index_hbm, index),
                (index_two_hbm, index_two),
                (w_self_hbm, w_self),
                (w_neigh_hbm, w_neigh),
                (bias_hbm, bias),
                (w_self_two_hbm, w_self_two),
                (w_neigh_two_hbm, w_neigh_two),
                (bias_two_hbm, bias_two),
                (values_hbm, values),
                (values_two_hbm, values_two),
            )
        )
    ]
    for load in loads:
        load.start()
    loads[0].wait()
    for h in range(2):
        sreq[:, h, :] = req[:, pl.ds(pl.multiple_of(c * HALF_CAP + h * 128, 128), 128)]
    rreq[me] = sreq[me]
    pl.semaphore_wait(barrier, GROUPS)

    def req_copy(s):
        p = lax.rem(me + s, GROUPS)
        return pltpu.make_async_remote_copy(
            src_ref=sreq.at[p],
            dst_ref=rreq.at[me],
            send_sem=req_send.at[s],
            recv_sem=req_recv.at[s],
            device_id=(p, c),
            device_id_type=MESH,
        )

    width = STORE // CHUNKS

    def half_copy(j):
        part = pl.ds(j * width, width)
        return pltpu.make_async_remote_copy(
            src_ref=store_hbm.at[:, part],
            dst_ref=cols.at[half, part],
            send_sem=half_send.at[j],
            recv_sem=half_recv.at[j],
            device_id=(me, sib),
            device_id_type=MESH,
        )

    half_copy(0).start()

    def req_start(s, _):
        req_copy(s).start()
        return 0

    lax.fori_loop(1, GROUPS, req_start, 0)
    for j in range(1, CHUNKS):
        half_copy(j).start()
    loads[1].wait()
    for j in range(CHUNKS):
        half_copy(j).wait_recv()
        part = pl.ds(j * width, width)
        rows[part, :] = cols[:, part].T.astype(f32)

    def req_wait(s, _):
        req_copy(s).wait_recv()
        return 0

    lax.fori_loop(1, GROUPS, req_wait, 0)
    idx_copy = pltpu.make_async_copy(rreq, idx, idx_sem)
    idx_copy.start()
    idx_copy.wait()

    def gather(p):
        for h in range(2):
            for q in range(128):
                tmp[pl.ds(h * 128 + q, 1), :] = rows[pl.ds(idx[p, h, q], 1), :]
        return tmp[...].astype(bf16).reshape(4, BLOCK, FEAT)

    def msg_copy(s):
        p = peer(me, s, c)
        return pltpu.make_async_remote_copy(
            src_ref=sendbuf.at[pl.ds(p * 4, 4)],
            dst_ref=rbuf.at[pl.ds(me * 4, 4)],
            send_sem=msg_send.at[s],
            recv_sem=msg_recv.at[s],
            device_id=(p, c),
            device_id_type=MESH,
        )

    def msg_start(i, _):
        s = shift_of(i)
        p = peer(me, s, c)
        sendbuf[pl.ds(p * 4, 4)] = gather(p)
        msg_copy(s).start()
        return 0

    lax.fori_loop(0, GROUPS - 1, msg_start, 0)
    rbuf[pl.ds(me * 4, 4)] = gather(me)

    for load in loads[2:]:
        load.wait()
    ones = jnp.ones((NBR * BLOCK, FEAT), bf16)

    def total(t, _):
        totals[t] = jnp.dot(values[c * OWN_TB + t], ones, preferred_element_type=f32)
        totals_two[t] = jnp.dot(values_two[t], ones, preferred_element_type=f32)
        return 0

    lax.fori_loop(0, OWN_TB, total, 0)
    spread = lax.broadcasted_iota(jnp.int32, (NBR, NBR * BLOCK), 1) // BLOCK
    spread = (spread == lax.broadcasted_iota(jnp.int32, (NBR, NBR * BLOCK), 0)).astype(f32)
    mine = (((index_vec[...] >> 2) & 1) == c).astype(f32)
    held[...] = lax.dot_general(
        mine, spread, (((0,), (0,)), ((), ())), preferred_element_type=f32
    )

    def mask(t, _):
        values[t] = values[t] * held[pl.ds(t, 1), :].astype(bf16)
        return 0

    lax.fori_loop(0, TB, mask, 0)

    def msg_wait(s, _):
        msg_copy(s).wait_recv()
        return 0

    lax.fori_loop(1, GROUPS, msg_wait, 0)

    def self_copy(j):
        return pltpu.make_async_remote_copy(
            src_ref=rbuf.at[pl.ds((sib * 4 + j) * 4, 4)],
            dst_ref=selfbuf.at[2 * j + c],
            send_sem=self_send.at[j],
            recv_sem=self_recv.at[j],
            device_id=(me, sib),
            device_id_type=MESH,
        )

    def self_local(j):
        return pltpu.make_async_copy(
            rbuf.at[pl.ds((c * 4 + j) * 4, 4)], selfbuf.at[2 * j + c], self_own.at[j]
        )

    for j in range(4):
        self_copy(j).start()
        self_local(j).start()

    def partial_sum(t):
        parts = []
        for k in range(NBR):
            b = index[k, t]
            parts.append(rbuf[(b >> 3) * 4 + (b & 3)])
        return jnp.dot(values[t], jnp.concatenate(parts, axis=0), preferred_element_type=f32)

    def p_copy(m):
        return pltpu.make_async_remote_copy(
            src_ref=psend.at[pl.ds(m * 8, 8)],
            dst_ref=precv.at[pl.ds(m * 8, 8)],
            send_sem=p_send.at[m],
            recv_sem=p_recv.at[m],
            device_id=(me, sib),
            device_id_type=MESH,
        )

    for m in range(4):
        for u in range(8):
            t = m * 8 + u
            psend[t] = partial_sum(sib * OWN_TB + t)
        p_copy(m).start()

    def own(i, _):
        for u in range(8):
            t = i * 8 + u
            agg[t] = partial_sum(c * OWN_TB + t)
        return 0

    lax.fori_loop(0, OWN_TB // 8, own, 0)

    def l1_copy(m):
        part = l1.at[pl.ds(c * OWN_TB + m * 4, 4)]
        return pltpu.make_async_remote_copy(
            src_ref=part,
            dst_ref=part,
            send_sem=l1_send.at[m],
            recv_sem=l1_recv.at[m],
            device_id=(me, sib),
            device_id_type=MESH,
        )

    def active(m):
        number = c * OWN_TB + m * 4 + lax.broadcasted_iota(jnp.int32, (256, HID), 0) // BLOCK
        return number < frontier[0]

    for j in range(4):
        self_copy(j).wait_recv()
        self_local(j).wait()
    for m in range(ROW_CHUNKS):
        if m % 2 == 0:
            p_copy(m // 2).wait_recv()
        mean = (agg[pl.ds(m * 4, 4)] + precv[pl.ds(m * 4, 4)]) / totals[pl.ds(m * 4, 4)]
        mean = mean.astype(bf16).reshape(256, FEAT)
        pre = (
            jnp.dot(selfbuf[m].reshape(256, FEAT), w_self[...], preferred_element_type=f32)
            + jnp.dot(mean, w_neigh[...], preferred_element_type=f32)
            + bias[...]
        )
        layer = jnp.where(active(m), jnp.maximum(pre, 0.0), 0.0).astype(bf16)
        l1[pl.ds(c * OWN_TB + m * 4, 4)] = layer.reshape(4, BLOCK, HID)
        l1_copy(m).start()

    def own_part(m, _):
        mine = l1[pl.ds(c * OWN_TB + m * 4, 4)].reshape(256, HID)
        pre_two[pl.ds(m * 4, 4)] = (
            jnp.dot(mine, w_self_two[...], preferred_element_type=f32) + bias_two[...]
        ).reshape(4, BLOCK, HID)
        return 0

    lax.fori_loop(0, ROW_CHUNKS, own_part, 0)
    for m in range(ROW_CHUNKS):
        l1_copy(m).wait_recv()

    def out_copy(m):
        at = pl.ds(m * 256, 256)
        return pltpu.make_async_copy(l2.at[at], out.at[at], out_sem.at[m])

    for m in range(ROW_CHUNKS):
        means = []
        for u in range(4):
            t = m * 4 + u
            parts = [l1[index_two[k, t]] for k in range(NBR)]
            summed = jnp.dot(
                values_two[t], jnp.concatenate(parts, axis=0), preferred_element_type=f32
            )
            total = jnp.concatenate([totals_two[t], totals_two[t]], axis=1)
            means.append((summed / total).astype(bf16))
        mean = jnp.concatenate(means, axis=0)
        pre = (
            jnp.dot(mean, w_neigh_two[...], preferred_element_type=f32)
            + pre_two[pl.ds(m * 4, 4)].reshape(256, HID)
        )
        layer = jnp.where(active(m), jnp.maximum(pre, 0.0), 0.0)
        l2[pl.ds(m * 256, 256), :] = layer.astype(bf16)
        out_copy(m).start()

    for m in range(ROW_CHUNKS):
        out_copy(m).wait()
        l1_copy(m).wait_send()
    for j in range(CHUNKS):
        half_copy(j).wait_send()
    for j in range(4):
        self_copy(j).wait_send()
        p_copy(j).wait_send()

    def sent(s, _):
        req_copy(s).wait_send()
        msg_copy(s).wait_send()
        return 0

    lax.fori_loop(1, GROUPS, sent, 0)


def body(
    feature_store,
    requests,
    block_index,
    block_values,
    frontier,
    self_first,
    neigh_first,
    bias_first,
    second_index,
    second_values,
    self_second,
    neigh_second,
    bias_second,
    classifier,
    bias_class,
):
    smem = pl.BlockSpec(memory_space=pltpu.SMEM)
    hbm = pl.BlockSpec(memory_space=pl.ANY)
    dma = pltpu.SemaphoreType.DMA
    bf16, f32, i32 = jnp.bfloat16, jnp.float32, jnp.int32
    layer_two = pl.pallas_call(
        kernel,
        out_shape=jax.ShapeDtypeStruct((OWN_TB * BLOCK, HID), bf16),
        in_specs=[hbm] * 4 + [smem] + [hbm] * 8,
        out_specs=hbm,
        scratch_shapes=[
            pltpu.VMEM((FEAT, STORE), bf16),
            pltpu.VMEM((STORE, FEAT), f32),
            pltpu.VMEM((GROUPS, 2 * HALF_CAP), i32),
            pltpu.VMEM((GROUPS, 2, 128), i32),
            pltpu.VMEM((GROUPS, 2, 128), i32),
            pltpu.SMEM((GROUPS, 2, 128), i32),
            pltpu.VMEM((NBR, TB), i32),
            pltpu.SMEM((NBR, TB), i32),
            pltpu.SMEM((NBR, OWN_TB), i32),
            pltpu.VMEM((HALF_CAP, FEAT), f32),
            pltpu.VMEM((GROUPS * 4, BLOCK, FEAT), bf16),
            pltpu.VMEM((GROUPS * 4, BLOCK, FEAT), bf16),
            pltpu.VMEM((TB, BLOCK, NBR * BLOCK), bf16),
            pltpu.VMEM((OWN_TB, BLOCK, NBR * BLOCK), bf16),
            pltpu.VMEM((TB, NBR * BLOCK), f32),
            pltpu.VMEM((FEAT, HID), bf16),
            pltpu.VMEM((FEAT, HID), bf16),
            pltpu.VMEM((1, HID), f32),
            pltpu.VMEM((HID, HID), bf16),
            pltpu.VMEM((HID, HID), bf16),
            pltpu.VMEM((1, HID), f32),
            pltpu.VMEM((OWN_TB, BLOCK, FEAT), f32),
            pltpu.VMEM((OWN_TB, BLOCK, FEAT), f32),
            pltpu.VMEM((OWN_TB, BLOCK, FEAT), f32),
            pltpu.VMEM((OWN_TB, BLOCK, FEAT), f32),
            pltpu.VMEM((8, 4, BLOCK, FEAT), bf16),
            pltpu.VMEM((OWN_TB, BLOCK, FEAT), f32),
            pltpu.VMEM((TB, BLOCK, HID), bf16),
            pltpu.VMEM((OWN_TB, BLOCK, HID), f32),
            pltpu.VMEM((OWN_TB * BLOCK, HID), bf16),
            dma((13,)),
            dma((CHUNKS,)),
            dma((CHUNKS,)),
            dma((GROUPS,)),
            dma((GROUPS,)),
            dma,
            dma((GROUPS,)),
            dma((GROUPS,)),
            dma((4,)),
            dma((4,)),
            dma((4,)),
            dma((4,)),
            dma((4,)),
            dma((ROW_CHUNKS,)),
            dma((ROW_CHUNKS,)),
            dma((ROW_CHUNKS,)),
        ],
        compiler_params=pltpu.CompilerParams(
            collective_id=0, has_side_effects=True, vmem_limit_bytes=60 * 2**20
        ),
        name="graph_layers",
    )(
        feature_store,
        requests,
        block_index.T,
        block_values,
        frontier,
        self_first,
        neigh_first,
        bias_first.reshape(1, HID),
        second_index.T,
        second_values,
        self_second,
        neigh_second,
        bias_second.reshape(1, HID),
    )
    return jnp.dot(layer_two, classifier, preferred_element_type=f32) + bias_class


def solution(mesh):
    in_specs = (
        P("feat", "batch"),
        P("batch", None),
        P("batch", None),
        P("batch", None, None),
        P("batch"),
        P(),
        P(),
        P(),
        P(("batch", "feat"), None),
        P(("batch", "feat"), None, None),
        P(),
        P(),
        P(),
        P(),
        P(),
    )
    out_specs = P(("batch", "feat"), None)
    return jax.shard_map(body, mesh=mesh, in_specs=in_specs, out_specs=out_specs, check_vma=False)
```

```python
import functools

import jax
import jax.numpy as jnp
from jax import lax
from jax.experimental import pallas as pl
from jax.experimental.pallas import tpu as pltpu
from jax.sharding import PartitionSpec as P

MESH = pl.DeviceIdType.MESH
BLOCK = 64
GROUPS = 64
HALF_CAP = 256
FEAT = 128
HID = 256
TB = 64
OWN_TB = 32
NBR = 8
STORE = 16384
CHUNKS = 4
ROW_CHUNKS = 8


ORDER = (
    42, 54, 28, 4, 46, 61, 23, 34, 8, 59, 17, 6, 44, 45, 7, 50,
    24, 29, 55, 30, 52, 47, 5, 13, 39, 58, 16, 1, 43, 62, 20, 2,
    40, 41, 3, 15, 37, 18, 56, 63, 21, 11, 33, 48, 26, 12, 38, 36,
    14, 53, 31, 22, 60, 10, 32, 35, 9, 19, 57, 51, 25, 27, 49,
)
WORDS = [
    sum(s * 64**e for e, s in enumerate(ORDER[w : w + 5])) for w in range(0, GROUPS - 1, 5)
]


def shift_of(i):
    word = jnp.int32(WORDS[0])
    for w in range(1, len(WORDS)):
        word = jnp.where(i // 5 == w, jnp.int32(WORDS[w]), word)
    place = lax.rem(i, 5)
    shift = lax.rem(word, 64)
    for e in range(1, 5):
        shift = jnp.where(place == e, lax.rem(word // 64**e, 64), shift)
    return shift


def peer(me, s, c):
    z, y, x = me // 16, (me // 4) % 4, me % 4
    dz, dy, dx = s // 16, (s // 4) % 4, s % 4
    dz, dy, dx = (lax.rem(d * (1 + 2 * c), 4) for d in (dz, dy, dx))
    return ((z + dz) % 4) * 16 + ((y + dy) % 4) * 4 + (x + dx) % 4


def kernel(
    store_hbm,
    req_hbm,
    index_hbm,
    values_hbm,
    frontier,
    w_self_hbm,
    w_neigh_hbm,
    bias_hbm,
    index_two_hbm,
    values_two_hbm,
    w_self_two_hbm,
    w_neigh_two_hbm,
    bias_two_hbm,
    out,
    cols,
    rows,
    req,
    sreq,
    rreq,
    idx,
    index_vec,
    index,
    index_two,
    tmp,
    sendbuf,
    rbuf,
    values,
    values_two,
    held,
    w_first,
    bias,
    w_self_two,
    w_neigh_two,
    bias_two,
    psend,
    precv,
    totals,
    totals_two,
    selfbuf,
    agg,
    l1,
    pre_two,
    l2,
    req_sem,
    own_sem,
    load_sem,
    half_send,
    half_recv,
    req_send,
    req_recv,
    idx_sem,
    msg_send,
    msg_recv,
    p_send,
    p_recv,
    self_send,
    self_recv,
    self_own,
    l1_send,
    l1_recv,
    out_sem,
):
    me = lax.axis_index("batch")
    c = lax.axis_index("feat")
    sib = 1 - c
    f32, bf16 = jnp.float32, jnp.bfloat16

    half = pl.ds(pl.multiple_of(c * 64, 64), 64)
    req_load = pltpu.make_async_copy(req_hbm, req, req_sem)
    req_load.start()
    own_load = pltpu.make_async_copy(store_hbm, cols.at[half], own_sem)
    own_load.start()
    barrier = pltpu.get_barrier_semaphore()
    pl.semaphore_signal(barrier, inc=1, device_id=(me, sib), device_id_type=MESH)

    def greet(s, _):
        pl.semaphore_signal(
            barrier, inc=1, device_id=(lax.rem(me + s, GROUPS), c), device_id_type=MESH
        )
        return 0

    lax.fori_loop(1, GROUPS, greet, 0)

    loads = [
        pltpu.make_async_copy(src, dst, load_sem.at[i])
        for i, (src, dst) in enumerate(
            (
                (index_hbm, index_vec),
                (index_hbm, index),
                (index_two_hbm, index_two),
                (w_self_hbm, w_first.at[pl.ds(0, FEAT)]),
                (w_neigh_hbm, w_first.at[pl.ds(FEAT, FEAT)]),
                (bias_hbm, bias),
                (w_self_two_hbm, w_self_two),
                (w_neigh_two_hbm, w_neigh_two),
                (bias_two_hbm, bias_two),
                (values_hbm, values),
                (values_two_hbm, values_two),
            )
        )
    ]
    req_load.wait()
    for h in range(2):
        sreq[:, h, :] = req[:, pl.ds(pl.multiple_of(c * HALF_CAP + h * 128, 128), 128)]
    rreq[me] = sreq[me]
    pl.semaphore_wait(barrier, GROUPS)

    def req_copy(s):
        p = lax.rem(me + s, GROUPS)
        return pltpu.make_async_remote_copy(
            src_ref=sreq.at[p],
            dst_ref=rreq.at[me],
            send_sem=req_send,
            recv_sem=req_recv,
            device_id=(p, c),
            device_id_type=MESH,
        )

    width = STORE // CHUNKS

    def half_copy(j):
        part = pl.ds(j * width, width)
        return pltpu.make_async_remote_copy(
            src_ref=store_hbm.at[:, part],
            dst_ref=cols.at[half, part],
            send_sem=half_send.at[j],
            recv_sem=half_recv.at[j],
            device_id=(me, sib),
            device_id_type=MESH,
        )

    half_copy(0).start()

    def req_start(s, _):
        req_copy(s).start()
        return 0

    lax.fori_loop(1, GROUPS, req_start, 0)
    for j in range(1, CHUNKS):
        half_copy(j).start()
    own_load.wait()
    for load in loads:
        load.start()

    def wait_all(ref, rows_in_all, sem):
        part = ref.at[pl.ds(0, rows_in_all)]
        pltpu.make_async_copy(part, part, sem).wait()

    idx_copy = pltpu.make_async_copy(rreq, idx, idx_sem)
    for j in range(CHUNKS):
        half_copy(j).wait_recv()
        part = pl.ds(j * width, width)
        rows[part, :] = cols[:, part].T.astype(f32)
        if j == CHUNKS - 2:
            wait_all(rreq, GROUPS - 1, req_recv)
            idx_copy.start()
    idx_copy.wait()

    def gather(p):
        for h in range(2):
            for q in range(128):
                tmp[pl.ds(h * 128 + q, 1), :] = rows[pl.ds(idx[p, h, q], 1), :]
        return tmp[...].astype(bf16).reshape(4, BLOCK, FEAT)

    def msg_copy(s):
        p = peer(me, s, c)
        return pltpu.make_async_remote_copy(
            src_ref=sendbuf.at[pl.ds(p * 4, 4)],
            dst_ref=rbuf.at[pl.ds(me * 4, 4)],
            send_sem=msg_send,
            recv_sem=msg_recv,
            device_id=(p, c),
            device_id_type=MESH,
        )

    def msg_start(i, _):
        s = shift_of(i)
        p = peer(me, s, c)
        sendbuf[pl.ds(p * 4, 4)] = gather(p)
        msg_copy(s).start()
        return 0

    lax.fori_loop(0, GROUPS - 1, msg_start, 0)
    rbuf[pl.ds(me * 4, 4)] = gather(me)

    for load in loads:
        load.wait()
    ones = jnp.ones((NBR * BLOCK, FEAT), bf16)

    def total(t, _):
        totals[t] = jnp.dot(values[c * OWN_TB + t], ones, preferred_element_type=f32)
        totals_two[t] = jnp.dot(values_two[t], ones, preferred_element_type=f32)
        return 0

    lax.fori_loop(0, OWN_TB, total, 0)
    spread = lax.broadcasted_iota(jnp.int32, (NBR, NBR * BLOCK), 1) // BLOCK
    spread = (spread == lax.broadcasted_iota(jnp.int32, (NBR, NBR * BLOCK), 0)).astype(f32)
    mine = (((index_vec[...] >> 2) & 1) == c).astype(f32)
    held[...] = lax.dot_general(
        mine, spread, (((0,), (0,)), ((), ())), preferred_element_type=f32
    )

    def mask(t, _):
        values[t] = values[t] * held[pl.ds(t, 1), :].astype(bf16)
        return 0

    lax.fori_loop(0, TB, mask, 0)
    wait_all(sreq, GROUPS - 1, req_send)
    for j in range(CHUNKS):
        half_copy(j).wait_send()
    wait_all(rbuf, (GROUPS - 1) * 4, msg_recv)

    def self_copy(j):
        return pltpu.make_async_remote_copy(
            src_ref=rbuf.at[pl.ds((sib * 4 + j) * 4, 4)],
            dst_ref=selfbuf.at[2 * j + c],
            send_sem=self_send.at[j],
            recv_sem=self_recv.at[j],
            device_id=(me, sib),
            device_id_type=MESH,
        )

    def self_local(j):
        return pltpu.make_async_copy(
            rbuf.at[pl.ds((c * 4 + j) * 4, 4)], selfbuf.at[2 * j + c], self_own.at[j]
        )

    for j in range(4):
        self_copy(j).start()
        self_local(j).start()

    def partial_sums(t):
        both = []
        for u in range(2):
            parts = []
            for k in range(NBR):
                b = index[k, t + u]
                parts.append(rbuf[(b >> 3) * 4 + (b & 3)])
            both.append(jnp.concatenate(parts, axis=0))
        product = jnp.dot(
            values[pl.ds(t, 2)].reshape(2 * BLOCK, NBR * BLOCK),
            jnp.concatenate(both, axis=1),
            preferred_element_type=f32,
        )
        return product[:BLOCK, :FEAT], product[BLOCK:, FEAT:]

    def p_copy(m):
        return pltpu.make_async_remote_copy(
            src_ref=psend.at[pl.ds(m * 8, 8)],
            dst_ref=precv.at[pl.ds(m * 8, 8)],
            send_sem=p_send.at[m],
            recv_sem=p_recv.at[m],
            device_id=(me, sib),
            device_id_type=MESH,
        )

    for m in range(4):
        for t in range(m * 8, m * 8 + 8, 2):
            psend[t], psend[t + 1] = partial_sums(sib * OWN_TB + t)
        p_copy(m).start()

    def own(i, _):
        for u in range(0, 8, 2):
            t = i * 8 + u
            agg[t], agg[t + 1] = partial_sums(c * OWN_TB + t)
        return 0

    lax.fori_loop(0, OWN_TB // 8, own, 0)

    def l1_copy(m):
        part = l1.at[pl.ds(c * OWN_TB + m * 4, 4)]
        return pltpu.make_async_remote_copy(
            src_ref=part,
            dst_ref=part,
            send_sem=l1_send.at[m],
            recv_sem=l1_recv.at[m],
            device_id=(me, sib),
            device_id_type=MESH,
        )

    def active(m):
        number = c * OWN_TB + m * 4 + lax.broadcasted_iota(jnp.int32, (256, HID), 0) // BLOCK
        return number < frontier[0]

    for j in range(4):
        self_copy(j).wait_recv()
        self_local(j).wait()
    for m in range(ROW_CHUNKS):
        if m % 2 == 0:
            p_copy(m // 2).wait_recv()
        mean = (agg[pl.ds(m * 4, 4)] + precv[pl.ds(m * 4, 4)]) / totals[pl.ds(m * 4, 4)]
        mean = mean.astype(bf16).reshape(256, FEAT)
        both = jnp.concatenate([selfbuf[m].reshape(256, FEAT), mean], axis=1)
        pre = jnp.dot(both, w_first[...], preferred_element_type=f32) + bias[...]
        layer = jnp.where(active(m), jnp.maximum(pre, 0.0), 0.0).astype(bf16)
        l1[pl.ds(c * OWN_TB + m * 4, 4)] = layer.reshape(4, BLOCK, HID)
        l1_copy(m).start()

    def own_part(m, _):
        mine = l1[pl.ds(c * OWN_TB + m * 4, 4)].reshape(256, HID)
        pre_two[pl.ds(m * 4, 4)] = (
            jnp.dot(mine, w_self_two[...], preferred_element_type=f32) + bias_two[...]
        ).reshape(4, BLOCK, HID)
        return 0

    lax.fori_loop(0, ROW_CHUNKS, own_part, 0)
    for m in range(ROW_CHUNKS):
        l1_copy(m).wait_recv()

    def out_copy(m):
        at = pl.ds(m * 256, 256)
        return pltpu.make_async_copy(l2.at[at], out.at[at], out_sem.at[m])

    for m in range(ROW_CHUNKS):
        means = []
        for u in range(4):
            t = m * 4 + u
            parts = [l1[index_two[k, t]] for k in range(NBR)]
            summed = jnp.dot(
                values_two[t], jnp.concatenate(parts, axis=0), preferred_element_type=f32
            )
            total = jnp.concatenate([totals_two[t], totals_two[t]], axis=1)
            means.append((summed / total).astype(bf16))
        mean = jnp.concatenate(means, axis=0)
        pre = (
            jnp.dot(mean, w_neigh_two[...], preferred_element_type=f32)
            + pre_two[pl.ds(m * 4, 4)].reshape(256, HID)
        )
        layer = jnp.where(active(m), jnp.maximum(pre, 0.0), 0.0)
        l2[pl.ds(m * 256, 256), :] = layer.astype(bf16)
        out_copy(m).start()

    for m in range(ROW_CHUNKS):
        out_copy(m).wait()
        l1_copy(m).wait_send()
    for j in range(4):
        self_copy(j).wait_send()
        p_copy(j).wait_send()
    wait_all(sendbuf, (GROUPS - 1) * 4, msg_send)


def body(
    feature_store,
    requests,
    block_index,
    block_values,
    frontier,
    self_first,
    neigh_first,
    bias_first,
    second_index,
    second_values,
    self_second,
    neigh_second,
    bias_second,
    classifier,
    bias_class,
):
    smem = pl.BlockSpec(memory_space=pltpu.SMEM)
    hbm = pl.BlockSpec(memory_space=pl.ANY)
    dma = pltpu.SemaphoreType.DMA
    bf16, f32, i32 = jnp.bfloat16, jnp.float32, jnp.int32
    layer_two = pl.pallas_call(
        kernel,
        out_shape=jax.ShapeDtypeStruct((OWN_TB * BLOCK, HID), bf16),
        in_specs=[hbm] * 4 + [smem] + [hbm] * 8,
        out_specs=hbm,
        scratch_shapes=[
            pltpu.VMEM((FEAT, STORE), bf16),
            pltpu.VMEM((STORE, FEAT), f32),
            pltpu.VMEM((GROUPS, 2 * HALF_CAP), i32),
            pltpu.VMEM((GROUPS, 2, 128), i32),
            pltpu.VMEM((GROUPS, 2, 128), i32),
            pltpu.SMEM((GROUPS, 2, 128), i32),
            pltpu.VMEM((NBR, TB), i32),
            pltpu.SMEM((NBR, TB), i32),
            pltpu.SMEM((NBR, OWN_TB), i32),
            pltpu.VMEM((HALF_CAP, FEAT), f32),
            pltpu.VMEM((GROUPS * 4, BLOCK, FEAT), bf16),
            pltpu.VMEM((GROUPS * 4, BLOCK, FEAT), bf16),
            pltpu.VMEM((TB, BLOCK, NBR * BLOCK), bf16),
            pltpu.VMEM((OWN_TB, BLOCK, NBR * BLOCK), bf16),
            pltpu.VMEM((TB, NBR * BLOCK), f32),
            pltpu.VMEM((2 * FEAT, HID), bf16),
            pltpu.VMEM((1, HID), f32),
            pltpu.VMEM((HID, HID), bf16),
            pltpu.VMEM((HID, HID), bf16),
            pltpu.VMEM((1, HID), f32),
            pltpu.VMEM((OWN_TB, BLOCK, FEAT), f32),
            pltpu.VMEM((OWN_TB, BLOCK, FEAT), f32),
            pltpu.VMEM((OWN_TB, BLOCK, FEAT), f32),
            pltpu.VMEM((OWN_TB, BLOCK, FEAT), f32),
            pltpu.VMEM((8, 4, BLOCK, FEAT), bf16),
            pltpu.VMEM((OWN_TB, BLOCK, FEAT), f32),
            pltpu.VMEM((TB, BLOCK, HID), bf16),
            pltpu.VMEM((OWN_TB, BLOCK, HID), f32),
            pltpu.VMEM((OWN_TB * BLOCK, HID), bf16),
            dma,
            dma,
            dma((11,)),
            dma((CHUNKS,)),
            dma((CHUNKS,)),
            dma,
            dma,
            dma,
            dma,
            dma,
            dma((4,)),
            dma((4,)),
            dma((4,)),
            dma((4,)),
            dma((4,)),
            dma((ROW_CHUNKS,)),
            dma((ROW_CHUNKS,)),
            dma((ROW_CHUNKS,)),
        ],
        compiler_params=pltpu.CompilerParams(
            collective_id=0, has_side_effects=True, vmem_limit_bytes=60 * 2**20
        ),
        name="graph_layers",
    )(
        feature_store,
        requests,
        block_index.T,
        block_values,
        frontier,
        self_first,
        neigh_first,
        bias_first.reshape(1, HID),
        second_index.T,
        second_values,
        self_second,
        neigh_second,
        bias_second.reshape(1, HID),
    )
    return jnp.dot(layer_two, classifier, preferred_element_type=f32) + bias_class


def solution(mesh):
    in_specs = (
        P("feat", "batch"),
        P("batch", None),
        P("batch", None),
        P("batch", None, None),
        P("batch"),
        P(),
        P(),
        P(),
        P(("batch", "feat"), None),
        P(("batch", "feat"), None, None),
        P(),
        P(),
        P(),
        P(),
        P(),
    )
    out_specs = P(("batch", "feat"), None)
    return jax.shard_map(body, mesh=mesh, in_specs=in_specs, out_specs=out_specs, check_vma=False)
```

```python
import functools

import jax
import jax.numpy as jnp
from jax import lax
from jax.experimental import pallas as pl
from jax.experimental.pallas import tpu as pltpu
from jax.sharding import PartitionSpec as P

MESH = pl.DeviceIdType.MESH
BLOCK = 64
GROUPS = 64
HALF_CAP = 256
FEAT = 128
HID = 256
TB = 64
OWN_TB = 32
NBR = 8
STORE = 16384
CHUNKS = 4
ROW_CHUNKS = 8


ORDER = (
    42, 54, 28, 4, 46, 61, 23, 34, 8, 59, 17, 6, 44, 45, 7, 50,
    24, 29, 55, 30, 52, 47, 5, 13, 39, 58, 16, 1, 43, 62, 20, 2,
    40, 41, 3, 15, 37, 18, 56, 63, 21, 11, 33, 48, 26, 12, 38, 36,
    14, 53, 31, 22, 60, 10, 32, 35, 9, 19, 57, 51, 25, 27, 49,
)
WORDS = [
    sum(s * 64**e for e, s in enumerate(ORDER[w : w + 5])) for w in range(0, GROUPS - 1, 5)
]


def shift_of(i):
    word = jnp.int32(WORDS[0])
    for w in range(1, len(WORDS)):
        word = jnp.where(i // 5 == w, jnp.int32(WORDS[w]), word)
    place = lax.rem(i, 5)
    shift = lax.rem(word, 64)
    for e in range(1, 5):
        shift = jnp.where(place == e, lax.rem(word // 64**e, 64), shift)
    return shift


def peer(me, s, c):
    z, y, x = me // 16, (me // 4) % 4, me % 4
    dz, dy, dx = s // 16, (s // 4) % 4, s % 4
    dz, dy, dx = (lax.rem(d * (1 + 2 * c), 4) for d in (dz, dy, dx))
    return ((z + dz) % 4) * 16 + ((y + dy) % 4) * 4 + (x + dx) % 4


def kernel(
    store_hbm,
    req_hbm,
    index_hbm,
    values_hbm,
    frontier,
    w_self_hbm,
    w_neigh_hbm,
    bias_hbm,
    index_two_hbm,
    values_two_hbm,
    w_self_two_hbm,
    w_neigh_two_hbm,
    bias_two_hbm,
    out,
    cols,
    rows,
    req,
    sreq,
    rreq,
    idx,
    index_vec,
    index,
    index_two,
    tmp,
    sendbuf,
    rbuf,
    values,
    values_two,
    held,
    w_first,
    bias,
    w_self_two,
    w_neigh_two,
    bias_two,
    psend,
    precv,
    totals,
    totals_two,
    selfbuf,
    agg,
    l1,
    pre_two,
    req_sem,
    own_sem,
    load_sem,
    half_send,
    half_recv,
    req_send,
    req_recv,
    idx_sem,
    msg_send,
    msg_recv,
    p_send,
    p_recv,
    self_send,
    self_recv,
    l1_send,
    l1_recv,
):
    me = lax.axis_index("batch")
    c = lax.axis_index("feat")
    sib = 1 - c
    f32, bf16 = jnp.float32, jnp.bfloat16

    half = pl.ds(pl.multiple_of(c * 64, 64), 64)
    req_load = pltpu.make_async_copy(req_hbm, req, req_sem)
    req_load.start()
    own_load = pltpu.make_async_copy(store_hbm, cols.at[half], own_sem)
    own_load.start()
    barrier = pltpu.get_barrier_semaphore()
    pl.semaphore_signal(barrier, inc=1, device_id=(me, sib), device_id_type=MESH)

    def greet(s, _):
        pl.semaphore_signal(
            barrier, inc=1, device_id=(lax.rem(me + s, GROUPS), c), device_id_type=MESH
        )
        return 0

    lax.fori_loop(1, GROUPS, greet, 0)

    loads = [
        pltpu.make_async_copy(src, dst, load_sem.at[i])
        for i, (src, dst) in enumerate(
            (
                (index_hbm, index_vec),
                (index_hbm, index),
                (index_two_hbm, index_two),
                (w_self_hbm, w_first.at[pl.ds(0, FEAT)]),
                (w_neigh_hbm, w_first.at[pl.ds(FEAT, FEAT)]),
                (bias_hbm, bias),
                (w_self_two_hbm, w_self_two),
                (w_neigh_two_hbm, w_neigh_two),
                (bias_two_hbm, bias_two),
                (values_hbm, values),
                (values_two_hbm, values_two),
            )
        )
    ]
    req_load.wait()
    for h in range(2):
        sreq[:, h, :] = req[:, pl.ds(pl.multiple_of(c * HALF_CAP + h * 128, 128), 128)]
    rreq[me] = sreq[me]
    pl.semaphore_wait(barrier, GROUPS)

    def req_copy(s):
        p = lax.rem(me + s, GROUPS)
        return pltpu.make_async_remote_copy(
            src_ref=sreq.at[p],
            dst_ref=rreq.at[me],
            send_sem=req_send,
            recv_sem=req_recv,
            device_id=(p, c),
            device_id_type=MESH,
        )

    width = STORE // CHUNKS

    def half_copy(j):
        part = pl.ds(j * width, width)
        return pltpu.make_async_remote_copy(
            src_ref=store_hbm.at[:, part],
            dst_ref=cols.at[half, part],
            send_sem=half_send.at[j],
            recv_sem=half_recv.at[j],
            device_id=(me, sib),
            device_id_type=MESH,
        )

    half_copy(0).start()

    def req_start(s, _):
        req_copy(s).start()
        return 0

    lax.fori_loop(1, GROUPS, req_start, 0)
    for j in range(1, CHUNKS):
        half_copy(j).start()
    own_load.wait()
    for load in loads:
        load.start()

    def wait_all(ref, rows_in_all, sem):
        part = ref.at[pl.ds(0, rows_in_all)]
        pltpu.make_async_copy(part, part, sem).wait()

    idx_copy = pltpu.make_async_copy(rreq, idx, idx_sem)
    for j in range(CHUNKS):
        half_copy(j).wait_recv()
        part = pl.ds(j * width, width)
        rows[part, :] = cols[:, part].T.astype(f32)
        if j == CHUNKS - 2:
            wait_all(rreq, GROUPS - 1, req_recv)
            idx_copy.start()
    idx_copy.wait()

    def gather(p):
        for h in range(2):
            for q in range(128):
                tmp[pl.ds(h * 128 + q, 1), :] = rows[pl.ds(idx[p, h, q], 1), :]
        return tmp[...].astype(bf16).reshape(4, BLOCK, FEAT)

    def msg_copy(s):
        p = peer(me, s, c)
        return pltpu.make_async_remote_copy(
            src_ref=sendbuf.at[pl.ds(p * 4, 4)],
            dst_ref=rbuf.at[pl.ds(me * 4, 4)],
            send_sem=msg_send,
            recv_sem=msg_recv,
            device_id=(p, c),
            device_id_type=MESH,
        )

    def msg_start(i, _):
        s = shift_of(i)
        p = peer(me, s, c)
        sendbuf[pl.ds(p * 4, 4)] = gather(p)
        msg_copy(s).start()
        return 0

    lax.fori_loop(0, GROUPS - 1, msg_start, 0)
    rbuf[pl.ds(me * 4, 4)] = gather(me)

    for load in loads:
        load.wait()
    ones = jnp.ones((NBR * BLOCK, FEAT), bf16)

    def total(t, _):
        totals[t] = jnp.dot(values[c * OWN_TB + t], ones, preferred_element_type=f32)
        totals_two[t] = jnp.dot(values_two[t], ones, preferred_element_type=f32)
        return 0

    lax.fori_loop(0, OWN_TB, total, 0)
    spread = lax.broadcasted_iota(jnp.int32, (NBR, NBR * BLOCK), 1) // BLOCK
    spread = (spread == lax.broadcasted_iota(jnp.int32, (NBR, NBR * BLOCK), 0)).astype(f32)
    mine = (((index_vec[...] >> 2) & 1) == c).astype(f32)
    held[...] = lax.dot_general(
        mine, spread, (((0,), (0,)), ((), ())), preferred_element_type=f32
    )

    def mask(t, _):
        values[t] = values[t] * held[pl.ds(t, 1), :].astype(bf16)
        return 0

    lax.fori_loop(0, TB, mask, 0)
    wait_all(sreq, GROUPS - 1, req_send)
    for j in range(CHUNKS):
        half_copy(j).wait_send()
    wait_all(rbuf, (GROUPS - 1) * 4, msg_recv)

    def self_copy(j):
        return pltpu.make_async_remote_copy(
            src_ref=rbuf.at[pl.ds((sib * 4 + j) * 4, 4)],
            dst_ref=selfbuf.at[2 * j + c],
            send_sem=self_send.at[j],
            recv_sem=self_recv.at[j],
            device_id=(me, sib),
            device_id_type=MESH,
        )

    for j in range(4):
        self_copy(j).start()

    for j in range(4):
        selfbuf[2 * j + c] = rbuf[pl.ds((c * 4 + j) * 4, 4)]

    def partial_sums(t):
        both = []
        for u in range(2):
            parts = []
            for k in range(NBR):
                b = index[k, t + u]
                parts.append(rbuf[(b >> 3) * 4 + (b & 3)])
            both.append(jnp.concatenate(parts, axis=0))
        product = jnp.dot(
            values[pl.ds(t, 2)].reshape(2 * BLOCK, NBR * BLOCK),
            jnp.concatenate(both, axis=1),
            preferred_element_type=f32,
        )
        return product[:BLOCK, :FEAT], product[BLOCK:, FEAT:]

    def p_copy(m):
        return pltpu.make_async_remote_copy(
            src_ref=psend.at[pl.ds(m * 8, 8)],
            dst_ref=precv.at[pl.ds(m * 8, 8)],
            send_sem=p_send.at[m],
            recv_sem=p_recv.at[m],
            device_id=(me, sib),
            device_id_type=MESH,
        )

    for m in range(4):
        for t in range(m * 8, m * 8 + 8, 2):
            psend[t], psend[t + 1] = partial_sums(sib * OWN_TB + t)
        p_copy(m).start()

    def own(i, _):
        for u in range(0, 8, 2):
            t = i * 8 + u
            agg[t], agg[t + 1] = partial_sums(c * OWN_TB + t)
        return 0

    lax.fori_loop(0, OWN_TB // 8, own, 0)

    def l1_copy(m):
        part = l1.at[pl.ds(c * OWN_TB + m * 4, 4)]
        return pltpu.make_async_remote_copy(
            src_ref=part,
            dst_ref=part,
            send_sem=l1_send.at[m],
            recv_sem=l1_recv.at[m],
            device_id=(me, sib),
            device_id_type=MESH,
        )

    def active(m):
        number = c * OWN_TB + m * 4 + lax.broadcasted_iota(jnp.int32, (256, HID), 0) // BLOCK
        return number < frontier[0]

    for j in range(4):
        self_copy(j).wait_recv()
    for m in range(ROW_CHUNKS):
        if m % 2 == 0:
            p_copy(m // 2).wait_recv()
        mean = (agg[pl.ds(m * 4, 4)] + precv[pl.ds(m * 4, 4)]) / totals[pl.ds(m * 4, 4)]
        mean = mean.astype(bf16).reshape(256, FEAT)
        both = jnp.concatenate([selfbuf[m].reshape(256, FEAT), mean], axis=1)
        pre = jnp.dot(both, w_first[...], preferred_element_type=f32) + bias[...]
        layer = jnp.where(active(m), jnp.maximum(pre, 0.0), 0.0).astype(bf16)
        l1[pl.ds(c * OWN_TB + m * 4, 4)] = layer.reshape(4, BLOCK, HID)
        l1_copy(m).start()

    def own_part(m, _):
        mine = l1[pl.ds(c * OWN_TB + m * 4, 4)].reshape(256, HID)
        pre_two[pl.ds(m * 4, 4)] = (
            jnp.dot(mine, w_self_two[...], preferred_element_type=f32) + bias_two[...]
        ).reshape(4, BLOCK, HID)
        return 0

    lax.fori_loop(0, ROW_CHUNKS, own_part, 0)
    for m in range(ROW_CHUNKS):
        l1_copy(m).wait_recv()

    for m in range(ROW_CHUNKS):
        means = []
        for u in range(4):
            t = m * 4 + u
            parts = [l1[index_two[k, t]] for k in range(NBR)]
            summed = jnp.dot(
                values_two[t], jnp.concatenate(parts, axis=0), preferred_element_type=f32
            )
            total = jnp.concatenate([totals_two[t], totals_two[t]], axis=1)
            means.append((summed / total).astype(bf16))
        mean = jnp.concatenate(means, axis=0)
        pre = (
            jnp.dot(mean, w_neigh_two[...], preferred_element_type=f32)
            + pre_two[pl.ds(m * 4, 4)].reshape(256, HID)
        )
        layer = jnp.where(active(m), jnp.maximum(pre, 0.0), 0.0)
        out[pl.ds(m * 256, 256), :] = layer.astype(bf16)

    for m in range(ROW_CHUNKS):
        l1_copy(m).wait_send()
    for j in range(4):
        self_copy(j).wait_send()
        p_copy(j).wait_send()
    wait_all(sendbuf, (GROUPS - 1) * 4, msg_send)


def body(
    feature_store,
    requests,
    block_index,
    block_values,
    frontier,
    self_first,
    neigh_first,
    bias_first,
    second_index,
    second_values,
    self_second,
    neigh_second,
    bias_second,
    classifier,
    bias_class,
):
    smem = pl.BlockSpec(memory_space=pltpu.SMEM)
    hbm = pl.BlockSpec(memory_space=pl.ANY)
    dma = pltpu.SemaphoreType.DMA
    bf16, f32, i32 = jnp.bfloat16, jnp.float32, jnp.int32
    layer_two = pl.pallas_call(
        kernel,
        out_shape=pltpu.VMEM((OWN_TB * BLOCK, HID), bf16),
        in_specs=[hbm] * 4 + [smem] + [hbm] * 8,
        out_specs=pl.BlockSpec(memory_space=pltpu.VMEM),
        scratch_shapes=[
            pltpu.VMEM((FEAT, STORE), bf16),
            pltpu.VMEM((STORE, FEAT), f32),
            pltpu.VMEM((GROUPS, 2 * HALF_CAP), i32),
            pltpu.VMEM((GROUPS, 2, 128), i32),
            pltpu.VMEM((GROUPS, 2, 128), i32),
            pltpu.SMEM((GROUPS, 2, 128), i32),
            pltpu.VMEM((NBR, TB), i32),
            pltpu.SMEM((NBR, TB), i32),
            pltpu.SMEM((NBR, OWN_TB), i32),
            pltpu.VMEM((HALF_CAP, FEAT), f32),
            pltpu.VMEM((GROUPS * 4, BLOCK, FEAT), bf16),
            pltpu.VMEM((GROUPS * 4, BLOCK, FEAT), bf16),
            pltpu.VMEM((TB, BLOCK, NBR * BLOCK), bf16),
            pltpu.VMEM((OWN_TB, BLOCK, NBR * BLOCK), bf16),
            pltpu.VMEM((TB, NBR * BLOCK), f32),
            pltpu.VMEM((2 * FEAT, HID), bf16),
            pltpu.VMEM((1, HID), f32),
            pltpu.VMEM((HID, HID), bf16),
            pltpu.VMEM((HID, HID), bf16),
            pltpu.VMEM((1, HID), f32),
            pltpu.VMEM((OWN_TB, BLOCK, FEAT), f32),
            pltpu.VMEM((OWN_TB, BLOCK, FEAT), f32),
            pltpu.VMEM((OWN_TB, BLOCK, FEAT), f32),
            pltpu.VMEM((OWN_TB, BLOCK, FEAT), f32),
            pltpu.VMEM((8, 4, BLOCK, FEAT), bf16),
            pltpu.VMEM((OWN_TB, BLOCK, FEAT), f32),
            pltpu.VMEM((TB, BLOCK, HID), bf16),
            pltpu.VMEM((OWN_TB, BLOCK, HID), f32),
            dma,
            dma,
            dma((11,)),
            dma((CHUNKS,)),
            dma((CHUNKS,)),
            dma,
            dma,
            dma,
            dma,
            dma,
            dma((4,)),
            dma((4,)),
            dma((4,)),
            dma((4,)),
            dma((ROW_CHUNKS,)),
            dma((ROW_CHUNKS,)),
        ],
        compiler_params=pltpu.CompilerParams(
            collective_id=0, has_side_effects=True, vmem_limit_bytes=58 * 2**20
        ),
        name="graph_layers",
    )(
        feature_store,
        requests,
        block_index.T,
        block_values,
        frontier,
        self_first,
        neigh_first,
        bias_first.reshape(1, HID),
        second_index.T,
        second_values,
        self_second,
        neigh_second,
        bias_second.reshape(1, HID),
    )
    return jnp.dot(layer_two, classifier, preferred_element_type=f32) + bias_class


def solution(mesh):
    in_specs = (
        P("feat", "batch"),
        P("batch", None),
        P("batch", None),
        P("batch", None, None),
        P("batch"),
        P(),
        P(),
        P(),
        P(("batch", "feat"), None),
        P(("batch", "feat"), None, None),
        P(),
        P(),
        P(),
        P(),
        P(),
    )
    out_specs = P(("batch", "feat"), None)
    return jax.shard_map(body, mesh=mesh, in_specs=in_specs, out_specs=out_specs, check_vma=False)
```

```python
import functools

import jax
import jax.numpy as jnp
from jax import lax
from jax.experimental import pallas as pl
from jax.experimental.pallas import tpu as pltpu
from jax.sharding import PartitionSpec as P

MESH = pl.DeviceIdType.MESH
BLOCK = 64
GROUPS = 64
HALF_CAP = 256
FEAT = 128
HID = 256
TB = 64
OWN_TB = 32
NBR = 8
STORE = 16384
CHUNKS = 4
ROW_CHUNKS = 8
PARTS = 4
PART_TB = OWN_TB // PARTS
PART_ROWS = PART_TB * BLOCK


ORDER = (
    42, 41, 2, 43, 46, 52, 26, 58, 20, 34, 60, 27, 49, 10, 17, 59,
    19, 45, 5, 39, 15, 40, 13, 38, 62, 23, 57, 28, 54, 32, 25, 51,
    22, 8, 47, 18, 56, 9, 33, 7, 30, 63, 37, 11, 29, 53, 35, 50,
    24, 21, 44, 14, 55, 36, 31, 6, 61, 16, 4, 1, 12, 48, 3,
)
WORDS = [
    sum(s * 64**e for e, s in enumerate(ORDER[w : w + 5])) for w in range(0, GROUPS - 1, 5)
]


def shift_of(i):
    word = jnp.int32(WORDS[0])
    for w in range(1, len(WORDS)):
        word = jnp.where(i // 5 == w, jnp.int32(WORDS[w]), word)
    place = lax.rem(i, 5)
    shift = lax.rem(word, 64)
    for e in range(1, 5):
        shift = jnp.where(place == e, lax.rem(word // 64**e, 64), shift)
    return shift


def peer(me, s, c):
    z, y, x = me // 16, (me // 4) % 4, me % 4
    dz, dy, dx = s // 16, (s // 4) % 4, s % 4
    dz, dy, dx = (lax.rem(d * (1 + 2 * c), 4) for d in (dz, dy, dx))
    return ((z + dz) % 4) * 16 + ((y + dy) % 4) * 4 + (x + dx) % 4


def kernel(
    store_hbm,
    req_hbm,
    index_hbm,
    values_hbm,
    frontier_hbm,
    w_self_hbm,
    w_neigh_hbm,
    bias_hbm,
    index_two_hbm,
    values_two_hbm,
    w_self_two_hbm,
    w_neigh_two_hbm,
    bias_two_hbm,
    out,
    cols,
    rows,
    req,
    sreq,
    rreq,
    idx,
    index_vec,
    index,
    index_two,
    frontier,
    tmp,
    sendbuf,
    rbuf,
    values,
    values_two,
    held,
    w_first,
    bias,
    w_self_two,
    w_neigh_two,
    bias_two,
    psend,
    precv,
    totals,
    totals_two,
    selfbuf,
    agg,
    l1,
    pre_two,
    req_sem,
    own_sem,
    load_sem,
    half_send,
    half_recv,
    req_send,
    req_recv,
    idx_sem,
    msg_send,
    msg_recv,
    p_send,
    p_recv,
    self_send,
    self_recv,
    l1_send,
    l1_recv,
):
    me = lax.axis_index("batch")
    c = lax.axis_index("feat")
    sib = 1 - c
    f32, bf16 = jnp.float32, jnp.bfloat16

    half = pl.ds(pl.multiple_of(c * 64, 64), 64)
    req_load = pltpu.make_async_copy(req_hbm, req, req_sem)
    req_load.start()
    own_load = pltpu.make_async_copy(store_hbm, cols.at[half], own_sem)
    own_load.start()
    barrier = pltpu.get_barrier_semaphore()
    pl.semaphore_signal(barrier, inc=1, device_id=(me, sib), device_id_type=MESH)

    def greet(s, _):
        pl.semaphore_signal(
            barrier, inc=1, device_id=(lax.rem(me + s, GROUPS), c), device_id_type=MESH
        )
        return 0

    lax.fori_loop(1, GROUPS, greet, 0)

    loads = [
        pltpu.make_async_copy(src, dst, load_sem.at[i])
        for i, (src, dst) in enumerate(
            (
                (index_hbm, index_vec),
                (index_hbm, index),
                (index_two_hbm, index_two),
                (frontier_hbm, frontier),
                (w_self_hbm, w_first.at[pl.ds(0, FEAT)]),
                (w_neigh_hbm, w_first.at[pl.ds(FEAT, FEAT)]),
                (bias_hbm, bias),
                (w_self_two_hbm, w_self_two),
                (w_neigh_two_hbm, w_neigh_two),
                (bias_two_hbm, bias_two),
                (values_hbm, values),
                (values_two_hbm, values_two),
            )
        )
    ]
    req_load.wait()
    for h in range(2):
        sreq[:, h, :] = req[:, pl.ds(pl.multiple_of(c * HALF_CAP + h * 128, 128), 128)]
    rreq[me] = sreq[me]
    pl.semaphore_wait(barrier, GROUPS)

    def req_copy(s):
        p = lax.rem(me + s, GROUPS)
        return pltpu.make_async_remote_copy(
            src_ref=sreq.at[p],
            dst_ref=rreq.at[me],
            send_sem=req_send,
            recv_sem=req_recv,
            device_id=(p, c),
            device_id_type=MESH,
        )

    width = STORE // CHUNKS

    def half_copy(j):
        part = pl.ds(j * width, width)
        return pltpu.make_async_remote_copy(
            src_ref=store_hbm.at[:, part],
            dst_ref=cols.at[half, part],
            send_sem=half_send.at[j],
            recv_sem=half_recv.at[j],
            device_id=(me, sib),
            device_id_type=MESH,
        )

    half_copy(0).start()

    def req_start(s, _):
        req_copy(s).start()
        return 0

    lax.fori_loop(1, GROUPS, req_start, 0)
    for j in range(1, CHUNKS):
        half_copy(j).start()
    own_load.wait()
    for load in loads:
        load.start()

    def wait_all(ref, rows_in_all, sem):
        part = ref.at[pl.ds(0, rows_in_all)]
        pltpu.make_async_copy(part, part, sem).wait()

    idx_copy = pltpu.make_async_copy(rreq, idx, idx_sem)
    for j in range(CHUNKS):
        half_copy(j).wait_recv()
        part = pl.ds(j * width, width)
        rows[part, :] = cols[:, part].T.astype(f32)
        if j == CHUNKS - 2:
            wait_all(rreq, GROUPS - 1, req_recv)
            idx_copy.start()
    idx_copy.wait()

    def gather(p):
        for h in range(2):
            for q in range(128):
                tmp[pl.ds(h * 128 + q, 1), :] = rows[pl.ds(idx[p, h, q], 1), :]
        return tmp[...].astype(bf16).reshape(4, BLOCK, FEAT)

    def msg_copy(s):
        p = peer(me, s, c)
        return pltpu.make_async_remote_copy(
            src_ref=sendbuf.at[pl.ds(p * 4, 4)],
            dst_ref=rbuf.at[pl.ds(me * 4, 4)],
            send_sem=msg_send,
            recv_sem=msg_recv,
            device_id=(p, c),
            device_id_type=MESH,
        )

    def msg_start(i, _):
        s = shift_of(i)
        p = peer(me, s, c)
        sendbuf[pl.ds(p * 4, 4)] = gather(p)
        msg_copy(s).start()
        return 0

    lax.fori_loop(0, GROUPS - 1, msg_start, 0)
    rbuf[pl.ds(me * 4, 4)] = gather(me)

    for load in loads:
        load.wait()
    ones = jnp.ones((NBR * BLOCK, FEAT), bf16)

    def total(t, _):
        totals[t] = jnp.dot(values[c * OWN_TB + t], ones, preferred_element_type=f32)
        totals_two[t] = jnp.dot(values_two[t], ones, preferred_element_type=f32)
        return 0

    lax.fori_loop(0, OWN_TB, total, 0)
    spread = lax.broadcasted_iota(jnp.int32, (NBR, NBR * BLOCK), 1) // BLOCK
    spread = (spread == lax.broadcasted_iota(jnp.int32, (NBR, NBR * BLOCK), 0)).astype(f32)
    mine = (((index_vec[...] >> 2) & 1) == c).astype(f32)
    held[...] = lax.dot_general(
        mine, spread, (((0,), (0,)), ((), ())), preferred_element_type=f32
    )

    def mask(t, _):
        values[t] = values[t] * held[pl.ds(t, 1), :].astype(bf16)
        return 0

    lax.fori_loop(0, TB, mask, 0)
    wait_all(sreq, GROUPS - 1, req_send)
    for j in range(CHUNKS):
        half_copy(j).wait_send()
    wait_all(rbuf, (GROUPS - 1) * 4, msg_recv)

    def self_copy(j):
        return pltpu.make_async_remote_copy(
            src_ref=rbuf.at[pl.ds((sib * 4 + j) * 4, 4)],
            dst_ref=selfbuf.at[2 * j + c],
            send_sem=self_send.at[j],
            recv_sem=self_recv.at[j],
            device_id=(me, sib),
            device_id_type=MESH,
        )

    for j in range(4):
        self_copy(j).start()

    for j in range(4):
        selfbuf[2 * j + c] = rbuf[pl.ds((c * 4 + j) * 4, 4)]

    def partial_sums(t):
        both = []
        for u in range(2):
            parts = []
            for k in range(NBR):
                b = index[k, t + u]
                parts.append(rbuf[(b >> 3) * 4 + (b & 3)])
            both.append(jnp.concatenate(parts, axis=0))
        product = jnp.dot(
            values[pl.ds(t, 2)].reshape(2 * BLOCK, NBR * BLOCK),
            jnp.concatenate(both, axis=1),
            preferred_element_type=f32,
        )
        return product[:BLOCK, :FEAT], product[BLOCK:, FEAT:]

    def p_copy(m):
        return pltpu.make_async_remote_copy(
            src_ref=psend.at[pl.ds(m * 8, 8)],
            dst_ref=precv.at[pl.ds(m * 8, 8)],
            send_sem=p_send.at[m],
            recv_sem=p_recv.at[m],
            device_id=(me, sib),
            device_id_type=MESH,
        )

    for m in range(4):
        for t in range(m * 8, m * 8 + 8, 2):
            psend[t], psend[t + 1] = partial_sums(sib * OWN_TB + t)
        p_copy(m).start()

    def own(i, _):
        for u in range(0, 8, 2):
            t = i * 8 + u
            agg[t], agg[t + 1] = partial_sums(c * OWN_TB + t)
        return 0

    lax.fori_loop(0, OWN_TB // 8, own, 0)

    def l1_copy(m):
        part = l1.at[pl.ds(c * OWN_TB + m * PART_TB, PART_TB)]
        return pltpu.make_async_remote_copy(
            src_ref=part,
            dst_ref=part,
            send_sem=l1_send.at[m],
            recv_sem=l1_recv.at[m],
            device_id=(me, sib),
            device_id_type=MESH,
        )

    def active(first, count):
        rows_here = lax.broadcasted_iota(jnp.int32, (count * BLOCK, HID), 0) // BLOCK
        return c * OWN_TB + first + rows_here < frontier[0]

    for j in range(4):
        self_copy(j).wait_recv()
    for m in range(PARTS):
        for j in range(m * 4 // PARTS, (m + 1) * 4 // PARTS):
            p_copy(j).wait_recv()
        part = pl.ds(m * PART_TB, PART_TB)
        mean = ((agg[part] + precv[part]) / totals[part]).astype(bf16).reshape(PART_ROWS, FEAT)
        mine = selfbuf[pl.ds(m * 8 // PARTS, 8 // PARTS)].reshape(PART_ROWS, FEAT)
        both = jnp.concatenate([mine, mean], axis=1)
        pre = jnp.dot(both, w_first[...], preferred_element_type=f32) + bias[...]
        layer = jnp.where(active(m * PART_TB, PART_TB), jnp.maximum(pre, 0.0), 0.0).astype(bf16)
        l1[pl.ds(c * OWN_TB + m * PART_TB, PART_TB)] = layer.reshape(PART_TB, BLOCK, HID)
        l1_copy(m).start()

    def own_part(m, _):
        mine = l1[pl.ds(c * OWN_TB + m * 4, 4)].reshape(256, HID)
        pre_two[pl.ds(m * 4, 4)] = (
            jnp.dot(mine, w_self_two[...], preferred_element_type=f32) + bias_two[...]
        ).reshape(4, BLOCK, HID)
        return 0

    lax.fori_loop(0, ROW_CHUNKS, own_part, 0)
    for m in range(PARTS):
        l1_copy(m).wait_recv()

    for m in range(ROW_CHUNKS):
        means = []
        for u in range(4):
            t = m * 4 + u
            parts = [l1[index_two[k, t]] for k in range(NBR)]
            summed = jnp.dot(
                values_two[t], jnp.concatenate(parts, axis=0), preferred_element_type=f32
            )
            total = jnp.concatenate([totals_two[t], totals_two[t]], axis=1)
            means.append((summed / total).astype(bf16))
        mean = jnp.concatenate(means, axis=0)
        pre = (
            jnp.dot(mean, w_neigh_two[...], preferred_element_type=f32)
            + pre_two[pl.ds(m * 4, 4)].reshape(256, HID)
        )
        layer = jnp.where(active(m * 4, 4), jnp.maximum(pre, 0.0), 0.0)
        out[pl.ds(m * 256, 256), :] = layer.astype(bf16)

    for m in range(PARTS):
        l1_copy(m).wait_send()
    for j in range(4):
        self_copy(j).wait_send()
        p_copy(j).wait_send()
    wait_all(sendbuf, (GROUPS - 1) * 4, msg_send)


def body(
    feature_store,
    requests,
    block_index,
    block_values,
    frontier,
    self_first,
    neigh_first,
    bias_first,
    second_index,
    second_values,
    self_second,
    neigh_second,
    bias_second,
    classifier,
    bias_class,
):
    hbm = pl.BlockSpec(memory_space=pl.ANY)
    dma = pltpu.SemaphoreType.DMA
    bf16, f32, i32 = jnp.bfloat16, jnp.float32, jnp.int32
    layer_two = pl.pallas_call(
        kernel,
        out_shape=pltpu.VMEM((OWN_TB * BLOCK, HID), bf16),
        in_specs=[hbm] * 13,
        out_specs=pl.BlockSpec(memory_space=pltpu.VMEM),
        scratch_shapes=[
            pltpu.VMEM((FEAT, STORE), bf16),
            pltpu.VMEM((STORE, FEAT), f32),
            pltpu.VMEM((GROUPS, 2 * HALF_CAP), i32),
            pltpu.VMEM((GROUPS, 2, 128), i32),
            pltpu.VMEM((GROUPS, 2, 128), i32),
            pltpu.SMEM((GROUPS, 2, 128), i32),
            pltpu.VMEM((NBR, TB), i32),
            pltpu.SMEM((NBR, TB), i32),
            pltpu.SMEM((NBR, OWN_TB), i32),
            pltpu.SMEM((1,), i32),
            pltpu.VMEM((HALF_CAP, FEAT), f32),
            pltpu.VMEM((GROUPS * 4, BLOCK, FEAT), bf16),
            pltpu.VMEM((GROUPS * 4, BLOCK, FEAT), bf16),
            pltpu.VMEM((TB, BLOCK, NBR * BLOCK), bf16),
            pltpu.VMEM((OWN_TB, BLOCK, NBR * BLOCK), bf16),
            pltpu.VMEM((TB, NBR * BLOCK), f32),
            pltpu.VMEM((2 * FEAT, HID), bf16),
            pltpu.VMEM((1, HID), f32),
            pltpu.VMEM((HID, HID), bf16),
            pltpu.VMEM((HID, HID), bf16),
            pltpu.VMEM((1, HID), f32),
            pltpu.VMEM((OWN_TB, BLOCK, FEAT), f32),
            pltpu.VMEM((OWN_TB, BLOCK, FEAT), f32),
            pltpu.VMEM((OWN_TB, BLOCK, FEAT), f32),
            pltpu.VMEM((OWN_TB, BLOCK, FEAT), f32),
            pltpu.VMEM((8, 4, BLOCK, FEAT), bf16),
            pltpu.VMEM((OWN_TB, BLOCK, FEAT), f32),
            pltpu.VMEM((TB, BLOCK, HID), bf16),
            pltpu.VMEM((OWN_TB, BLOCK, HID), f32),
            dma,
            dma,
            dma((12,)),
            dma((CHUNKS,)),
            dma((CHUNKS,)),
            dma,
            dma,
            dma,
            dma,
            dma,
            dma((4,)),
            dma((4,)),
            dma((4,)),
            dma((4,)),
            dma((PARTS,)),
            dma((PARTS,)),
        ],
        compiler_params=pltpu.CompilerParams(
            collective_id=0, has_side_effects=True, vmem_limit_bytes=58 * 2**20
        ),
        name="graph_layers",
    )(
        feature_store,
        requests,
        block_index.T,
        block_values,
        frontier,
        self_first,
        neigh_first,
        bias_first.reshape(1, HID),
        second_index.T,
        second_values,
        self_second,
        neigh_second,
        bias_second.reshape(1, HID),
    )
    return jnp.dot(layer_two, classifier, preferred_element_type=f32) + bias_class


def solution(mesh):
    in_specs = (
        P("feat", "batch"),
        P("batch", None),
        P("batch", None),
        P("batch", None, None),
        P("batch"),
        P(),
        P(),
        P(),
        P(("batch", "feat"), None),
        P(("batch", "feat"), None, None),
        P(),
        P(),
        P(),
        P(),
        P(),
    )
    out_specs = P(("batch", "feat"), None)
    return jax.shard_map(body, mesh=mesh, in_specs=in_specs, out_specs=out_specs, check_vma=False)
```

```python
import functools

import jax
import jax.numpy as jnp
from jax import lax
from jax.experimental import pallas as pl
from jax.experimental.pallas import tpu as pltpu
from jax.sharding import PartitionSpec as P

MESH = pl.DeviceIdType.MESH
BLOCK = 64
GROUPS = 64
HALF_CAP = 256
FEAT = 128
HID = 256
TB = 64
OWN_TB = 32
NBR = 8
STORE = 16384
CHUNKS = 4
ROW_CHUNKS = 8
PARTS = 4
PART_TB = OWN_TB // PARTS
PART_ROWS = PART_TB * BLOCK


ORDER = (
    42, 41, 2, 43, 46, 52, 26, 58, 20, 34, 60, 27, 49, 10, 17, 59,
    19, 45, 5, 39, 15, 40, 13, 38, 62, 23, 57, 28, 54, 32, 25, 51,
    22, 8, 47, 18, 56, 9, 33, 7, 30, 63, 37, 11, 29, 53, 35, 50,
    24, 21, 44, 14, 55, 36, 31, 6, 61, 16, 4, 1, 12, 48, 3,
)
WORDS = [
    sum(s * 64**e for e, s in enumerate(ORDER[w : w + 5])) for w in range(0, GROUPS - 1, 5)
]


def shift_of(i):
    word = jnp.int32(WORDS[0])
    for w in range(1, len(WORDS)):
        word = jnp.where(i // 5 == w, jnp.int32(WORDS[w]), word)
    place = lax.rem(i, 5)
    shift = lax.rem(word, 64)
    for e in range(1, 5):
        shift = jnp.where(place == e, lax.rem(word // 64**e, 64), shift)
    return shift


def peer(me, s, c):
    z, y, x = me // 16, (me // 4) % 4, me % 4
    dz, dy, dx = s // 16, (s // 4) % 4, s % 4
    dz, dy, dx = (lax.rem(d * (1 + 2 * c), 4) for d in (dz, dy, dx))
    return ((z + dz) % 4) * 16 + ((y + dy) % 4) * 4 + (x + dx) % 4


def kernel(
    store_hbm,
    req_hbm,
    index_hbm,
    values_hbm,
    frontier_hbm,
    w_self_hbm,
    w_neigh_hbm,
    bias_hbm,
    index_two_hbm,
    values_two_hbm,
    w_self_two_hbm,
    w_neigh_two_hbm,
    bias_two_hbm,
    out,
    cols,
    rows,
    req,
    sreq,
    rreq,
    idx,
    index_vec,
    index,
    index_two,
    frontier,
    tmp,
    sendbuf,
    rbuf,
    values,
    values_two,
    held,
    w_first,
    bias,
    w_self_two,
    w_neigh_two,
    bias_two,
    psend,
    precv,
    inverse,
    inverse_two,
    selfbuf,
    agg,
    l1,
    pre_two,
    req_sem,
    own_sem,
    load_sem,
    half_send,
    half_recv,
    req_send,
    req_recv,
    idx_sem,
    msg_send,
    msg_recv,
    p_send,
    p_recv,
    self_send,
    self_recv,
    l1_send,
    l1_recv,
):
    me = lax.axis_index("batch")
    c = lax.axis_index("feat")
    sib = 1 - c
    f32, bf16 = jnp.float32, jnp.bfloat16

    half = pl.ds(pl.multiple_of(c * 64, 64), 64)
    req_load = pltpu.make_async_copy(req_hbm, req, req_sem)
    req_load.start()
    own_load = pltpu.make_async_copy(store_hbm, cols.at[half], own_sem)
    own_load.start()
    barrier = pltpu.get_barrier_semaphore()
    pl.semaphore_signal(barrier, inc=1, device_id=(me, sib), device_id_type=MESH)

    def greet(s, _):
        pl.semaphore_signal(
            barrier, inc=1, device_id=(lax.rem(me + s, GROUPS), c), device_id_type=MESH
        )
        return 0

    lax.fori_loop(1, GROUPS, greet, 0)

    loads = [
        pltpu.make_async_copy(src, dst, load_sem.at[i])
        for i, (src, dst) in enumerate(
            (
                (index_hbm, index_vec),
                (index_hbm, index),
                (index_two_hbm, index_two),
                (frontier_hbm, frontier),
                (w_self_hbm, w_first.at[pl.ds(0, FEAT)]),
                (w_neigh_hbm, w_first.at[pl.ds(FEAT, FEAT)]),
                (bias_hbm, bias),
                (w_self_two_hbm, w_self_two),
                (w_neigh_two_hbm, w_neigh_two),
                (bias_two_hbm, bias_two),
                (values_hbm, values),
                (values_two_hbm, values_two),
            )
        )
    ]
    req_load.wait()
    for h in range(2):
        sreq[:, h, :] = req[:, pl.ds(pl.multiple_of(c * HALF_CAP + h * 128, 128), 128)]
    rreq[me] = sreq[me]
    pl.semaphore_wait(barrier, GROUPS)

    def req_copy(s):
        p = lax.rem(me + s, GROUPS)
        return pltpu.make_async_remote_copy(
            src_ref=sreq.at[p],
            dst_ref=rreq.at[me],
            send_sem=req_send,
            recv_sem=req_recv,
            device_id=(p, c),
            device_id_type=MESH,
        )

    width = STORE // CHUNKS

    def half_copy(j):
        part = pl.ds(j * width, width)
        return pltpu.make_async_remote_copy(
            src_ref=store_hbm.at[:, part],
            dst_ref=cols.at[half, part],
            send_sem=half_send.at[j],
            recv_sem=half_recv.at[j],
            device_id=(me, sib),
            device_id_type=MESH,
        )

    half_copy(0).start()

    def req_start(s, _):
        req_copy(s).start()
        return 0

    lax.fori_loop(1, GROUPS, req_start, 0)
    for j in range(1, CHUNKS):
        half_copy(j).start()
    own_load.wait()
    for load in loads:
        load.start()

    def wait_all(ref, rows_in_all, sem):
        part = ref.at[pl.ds(0, rows_in_all)]
        pltpu.make_async_copy(part, part, sem).wait()

    idx_copy = pltpu.make_async_copy(rreq, idx, idx_sem)
    for j in range(CHUNKS):
        half_copy(j).wait_recv()
        part = pl.ds(j * width, width)
        rows[part, :] = cols[:, part].T.astype(f32)
        if j == CHUNKS - 2:
            wait_all(rreq, GROUPS - 1, req_recv)
            idx_copy.start()
    idx_copy.wait()

    def gather(p):
        for h in range(2):
            for q in range(128):
                tmp[pl.ds(h * 128 + q, 1), :] = rows[pl.ds(idx[p, h, q], 1), :]
        return tmp[...].astype(bf16).reshape(4, BLOCK, FEAT)

    def msg_copy(s):
        p = peer(me, s, c)
        return pltpu.make_async_remote_copy(
            src_ref=sendbuf.at[pl.ds(p * 4, 4)],
            dst_ref=rbuf.at[pl.ds(me * 4, 4)],
            send_sem=msg_send,
            recv_sem=msg_recv,
            device_id=(p, c),
            device_id_type=MESH,
        )

    def msg_start(i, _):
        s = shift_of(i)
        p = peer(me, s, c)
        sendbuf[pl.ds(p * 4, 4)] = gather(p)
        msg_copy(s).start()
        return 0

    lax.fori_loop(0, GROUPS - 1, msg_start, 0)
    rbuf[pl.ds(me * 4, 4)] = gather(me)

    for load in loads:
        load.wait()
    ones = jnp.ones((NBR * BLOCK, FEAT), bf16)

    def total(t, _):
        inverse[t] = 1.0 / jnp.dot(
            values[c * OWN_TB + t], ones, preferred_element_type=f32
        )
        inverse_two[t] = 1.0 / jnp.dot(values_two[t], ones, preferred_element_type=f32)
        return 0

    lax.fori_loop(0, OWN_TB, total, 0)
    spread = lax.broadcasted_iota(jnp.int32, (NBR, NBR * BLOCK), 1) // BLOCK
    spread = (spread == lax.broadcasted_iota(jnp.int32, (NBR, NBR * BLOCK), 0)).astype(f32)
    mine = (((index_vec[...] >> 2) & 1) == c).astype(f32)
    held[...] = lax.dot_general(
        mine, spread, (((0,), (0,)), ((), ())), preferred_element_type=f32
    )

    def mask(t, _):
        values[t] = values[t] * held[pl.ds(t, 1), :].astype(bf16)
        return 0

    lax.fori_loop(0, TB, mask, 0)
    wait_all(sreq, GROUPS - 1, req_send)
    for j in range(CHUNKS):
        half_copy(j).wait_send()
    wait_all(rbuf, (GROUPS - 1) * 4, msg_recv)

    def self_copy(j):
        return pltpu.make_async_remote_copy(
            src_ref=rbuf.at[pl.ds((sib * 4 + j) * 4, 4)],
            dst_ref=selfbuf.at[2 * j + c],
            send_sem=self_send.at[j],
            recv_sem=self_recv.at[j],
            device_id=(me, sib),
            device_id_type=MESH,
        )

    for j in range(4):
        self_copy(j).start()

    for j in range(4):
        selfbuf[2 * j + c] = rbuf[pl.ds((c * 4 + j) * 4, 4)]

    def partial_sums(t):
        both = []
        for u in range(2):
            parts = []
            for k in range(NBR):
                b = index[k, t + u]
                parts.append(rbuf[(b >> 3) * 4 + (b & 3)])
            both.append(jnp.concatenate(parts, axis=0))
        product = jnp.dot(
            values[pl.ds(t, 2)].reshape(2 * BLOCK, NBR * BLOCK),
            jnp.concatenate(both, axis=1),
            preferred_element_type=f32,
        )
        return product[:BLOCK, :FEAT], product[BLOCK:, FEAT:]

    def p_copy(m):
        return pltpu.make_async_remote_copy(
            src_ref=psend.at[pl.ds(m * 8, 8)],
            dst_ref=precv.at[pl.ds(m * 8, 8)],
            send_sem=p_send.at[m],
            recv_sem=p_recv.at[m],
            device_id=(me, sib),
            device_id_type=MESH,
        )

    for m in range(4):
        for t in range(m * 8, m * 8 + 8, 2):
            psend[t], psend[t + 1] = partial_sums(sib * OWN_TB + t)
        p_copy(m).start()

    def own(i, _):
        for u in range(0, 8, 2):
            t = i * 8 + u
            agg[t], agg[t + 1] = partial_sums(c * OWN_TB + t)
        return 0

    lax.fori_loop(0, OWN_TB // 8, own, 0)

    def l1_copy(m):
        part = l1.at[pl.ds(c * OWN_TB + m * PART_TB, PART_TB)]
        return pltpu.make_async_remote_copy(
            src_ref=part,
            dst_ref=part,
            send_sem=l1_send.at[m],
            recv_sem=l1_recv.at[m],
            device_id=(me, sib),
            device_id_type=MESH,
        )

    def active(first, count):
        rows_here = lax.broadcasted_iota(jnp.int32, (count * BLOCK, HID), 0) // BLOCK
        return c * OWN_TB + first + rows_here < frontier[0]

    for j in range(4):
        self_copy(j).wait_recv()
    for m in range(PARTS):
        for j in range(m * 4 // PARTS, (m + 1) * 4 // PARTS):
            p_copy(j).wait_recv()
        part = pl.ds(m * PART_TB, PART_TB)
        mean = ((agg[part] + precv[part]) * inverse[part]).astype(bf16).reshape(PART_ROWS, FEAT)
        mine = selfbuf[pl.ds(m * 8 // PARTS, 8 // PARTS)].reshape(PART_ROWS, FEAT)
        both = jnp.concatenate([mine, mean], axis=1)
        pre = jnp.dot(both, w_first[...], preferred_element_type=f32) + bias[...]
        layer = jnp.where(active(m * PART_TB, PART_TB), jnp.maximum(pre, 0.0), 0.0).astype(bf16)
        l1[pl.ds(c * OWN_TB + m * PART_TB, PART_TB)] = layer.reshape(PART_TB, BLOCK, HID)
        l1_copy(m).start()

    def own_part(m, _):
        mine = l1[pl.ds(c * OWN_TB + m * 4, 4)].reshape(256, HID)
        pre_two[pl.ds(m * 4, 4)] = (
            jnp.dot(mine, w_self_two[...], preferred_element_type=f32) + bias_two[...]
        ).reshape(4, BLOCK, HID)
        return 0

    lax.fori_loop(0, ROW_CHUNKS, own_part, 0)
    for m in range(PARTS):
        l1_copy(m).wait_recv()

    for m in range(ROW_CHUNKS):
        means = []
        for u in range(4):
            t = m * 4 + u
            parts = [l1[index_two[k, t]] for k in range(NBR)]
            summed = jnp.dot(
                values_two[t], jnp.concatenate(parts, axis=0), preferred_element_type=f32
            )
            total = jnp.concatenate([inverse_two[t], inverse_two[t]], axis=1)
            means.append((summed * total).astype(bf16))
        mean = jnp.concatenate(means, axis=0)
        pre = (
            jnp.dot(mean, w_neigh_two[...], preferred_element_type=f32)
            + pre_two[pl.ds(m * 4, 4)].reshape(256, HID)
        )
        layer = jnp.where(active(m * 4, 4), jnp.maximum(pre, 0.0), 0.0)
        out[pl.ds(m * 256, 256), :] = layer.astype(bf16)

    for m in range(PARTS):
        l1_copy(m).wait_send()
    for j in range(4):
        self_copy(j).wait_send()
        p_copy(j).wait_send()
    wait_all(sendbuf, (GROUPS - 1) * 4, msg_send)


def body(
    feature_store,
    requests,
    block_index,
    block_values,
    frontier,
    self_first,
    neigh_first,
    bias_first,
    second_index,
    second_values,
    self_second,
    neigh_second,
    bias_second,
    classifier,
    bias_class,
):
    hbm = pl.BlockSpec(memory_space=pl.ANY)
    dma = pltpu.SemaphoreType.DMA
    bf16, f32, i32 = jnp.bfloat16, jnp.float32, jnp.int32
    layer_two = pl.pallas_call(
        kernel,
        out_shape=pltpu.VMEM((OWN_TB * BLOCK, HID), bf16),
        in_specs=[hbm] * 13,
        out_specs=pl.BlockSpec(memory_space=pltpu.VMEM),
        scratch_shapes=[
            pltpu.VMEM((FEAT, STORE), bf16),
            pltpu.VMEM((STORE, FEAT), f32),
            pltpu.VMEM((GROUPS, 2 * HALF_CAP), i32),
            pltpu.VMEM((GROUPS, 2, 128), i32),
            pltpu.VMEM((GROUPS, 2, 128), i32),
            pltpu.SMEM((GROUPS, 2, 128), i32),
            pltpu.VMEM((NBR, TB), i32),
            pltpu.SMEM((NBR, TB), i32),
            pltpu.SMEM((NBR, OWN_TB), i32),
            pltpu.SMEM((1,), i32),
            pltpu.VMEM((HALF_CAP, FEAT), f32),
            pltpu.VMEM((GROUPS * 4, BLOCK, FEAT), bf16),
            pltpu.VMEM((GROUPS * 4, BLOCK, FEAT), bf16),
            pltpu.VMEM((TB, BLOCK, NBR * BLOCK), bf16),
            pltpu.VMEM((OWN_TB, BLOCK, NBR * BLOCK), bf16),
            pltpu.VMEM((TB, NBR * BLOCK), f32),
            pltpu.VMEM((2 * FEAT, HID), bf16),
            pltpu.VMEM((1, HID), f32),
            pltpu.VMEM((HID, HID), bf16),
            pltpu.VMEM((HID, HID), bf16),
            pltpu.VMEM((1, HID), f32),
            pltpu.VMEM((OWN_TB, BLOCK, FEAT), f32),
            pltpu.VMEM((OWN_TB, BLOCK, FEAT), f32),
            pltpu.VMEM((OWN_TB, BLOCK, FEAT), f32),
            pltpu.VMEM((OWN_TB, BLOCK, FEAT), f32),
            pltpu.VMEM((8, 4, BLOCK, FEAT), bf16),
            pltpu.VMEM((OWN_TB, BLOCK, FEAT), f32),
            pltpu.VMEM((TB, BLOCK, HID), bf16),
            pltpu.VMEM((OWN_TB, BLOCK, HID), f32),
            dma,
            dma,
            dma((12,)),
            dma((CHUNKS,)),
            dma((CHUNKS,)),
            dma,
            dma,
            dma,
            dma,
            dma,
            dma((4,)),
            dma((4,)),
            dma((4,)),
            dma((4,)),
            dma((PARTS,)),
            dma((PARTS,)),
        ],
        compiler_params=pltpu.CompilerParams(
            collective_id=0, has_side_effects=True, vmem_limit_bytes=58 * 2**20
        ),
        name="graph_layers",
    )(
        feature_store,
        requests,
        block_index.T,
        block_values,
        frontier,
        self_first,
        neigh_first,
        bias_first.reshape(1, HID),
        second_index.T,
        second_values,
        self_second,
        neigh_second,
        bias_second.reshape(1, HID),
    )
    return jnp.dot(layer_two, classifier, preferred_element_type=f32) + bias_class


def solution(mesh):
    in_specs = (
        P("feat", "batch"),
        P("batch", None),
        P("batch", None),
        P("batch", None, None),
        P("batch"),
        P(),
        P(),
        P(),
        P(("batch", "feat"), None),
        P(("batch", "feat"), None, None),
        P(),
        P(),
        P(),
        P(),
        P(),
    )
    out_specs = P(("batch", "feat"), None)
    return jax.shard_map(body, mesh=mesh, in_specs=in_specs, out_specs=out_specs, check_vma=False)
```
